512 devices in a mesh: region: 32 (over y, z_hi), member: 16 (over x, z_lo, core).
Axes of the slice: x: 4, y: 8, z: 8 (z_hi: 4, z_lo: 2; z = z_hi * 2 + z_lo), core: 2. Of those that a mesh axis runs over, the one named last changes fastest.
Arguments:
- ensemble: bfloat16 [256, 262144], P('member', 'region'), may hold values from -6 to 6
- reports: float32 [32, 1024], P('region'), may hold values from -6 to 6
- report_count: int32 [32], P('region'), may hold values from 128 to 1024, as said below
- report_cell: int32 [32, 1024], P('region'), may hold values from 0 to 262143, as said below
- report_weight: float32 [32, 64, 1024], P('region', 'member'), may hold values from 0.001 to 1
- blending: float32 [4, 262144], P(None, ('region', 'member')), may hold values from 0.02 to 1
Outputs:
- analysis: bfloat16 [262144, 256], P(('region', 'member'))
The draws below stay inside these ranges and needn't reach their ends.
Inputs may be any that keep to these rules, and one draw needn't show every extreme that they name: `report_count`: the largest value 1024 is reached by some region in every draw. `report_cell`: every cell lies in the slot's own region, or in the first 128 cells of one of at most two other regions chosen for that region.
All inputs are finite; a program needn't handle non-finite values.
Results may differ from the reference program's by a relative error of at most 0.0055.
Values may be sent and summed in bfloat16 or wider, within the bound.
A program may use at most 64 MiB of HBM per device.

```python
import math
import jax
import jax.numpy as jnp
from jax import lax

MEMBERS = 256
REPORTS = 1024
POINTS_DEV = 4
MARGIN = 128
SWEEPS = 4
REGIONS = 32
POINT_ROWS = 16
POINTS = 64
CELLS = 8192
ALL_CELLS = 262144


def draw_report_count(key, part):
    counts = jax.random.randint(key, (REGIONS,), REPORTS // 8, REPORTS + 1)
    fullest = jax.random.randint(jax.random.fold_in(key, 7), (), 0, REGIONS)
    return jnp.where(jnp.arange(REGIONS) == fullest, REPORTS, counts).astype(jnp.int32)


def draw_report_cell(key, part):
    streams = jax.random.split(jax.random.fold_in(key, 11), 5)
    first_pick = jax.random.randint(streams[0], (REGIONS,), 0, REGIONS - 1)
    second_pick = jax.random.randint(streams[1], (REGIONS,), 0, REGIONS - 2)
    region = jnp.arange(REGIONS)
    source_one = (region + 1 + first_pick) % REGIONS
    source_two = (region + 1 + (first_pick + 1 + second_pick) % (REGIONS - 1)) % REGIONS
    kinds = jax.random.randint(streams[2], (REGIONS, REPORTS), 0, 4)
    home_cell = jax.random.randint(streams[3], (REGIONS, REPORTS), 0, CELLS)
    edge_cell = jax.random.randint(streams[4], (REGIONS, REPORTS), 0, MARGIN)
    holder = jnp.where(kinds == 2, source_one[:, None], jnp.where(kinds == 3, source_two[:, None], region[:, None]))
    placed = jnp.where(kinds >= 2, edge_cell, home_cell)
    result = holder * CELLS + placed
    position = jnp.arange(REPORTS)[None, :]
    result = jnp.where((region[:, None] == REGIONS - 1) & (position == 0), REGIONS * CELLS - 1, result)
    result = jnp.where((region[:, None] == 0) & (position == 0), 0, result)
    return result.astype(jnp.int32)


def block_levels(stream_key, extent, shards, low, top_value):
    gain = 1.0
    for dim, blocks in shards:
        draws = jax.random.uniform(jax.random.fold_in(jax.random.fold_in(stream_key, 6), dim), (blocks,), jnp.float32, low / len(shards), top_value / len(shards))
        gain = gain * jnp.repeat(jnp.exp(draws), extent[dim] // blocks).reshape((-1,) + (1,) * (len(extent) - 1 - dim))
    return gain


def scatter_about(own_key, extent, scale, limit, pieces=(), kind=jnp.bfloat16):
    drawn = scale * jax.random.normal(own_key, extent, jnp.float32)
    if pieces:
        drawn = drawn * block_levels(own_key, extent, pieces, -0.22, 0.18)
    return jnp.clip(drawn, -limit, limit).astype(kind)


def setup_inputs(seed: int = 0) -> dict:
    arg_keys = jax.random.split(jax.random.key(seed), 7)
    ensemble = scatter_about(arg_keys[0], (MEMBERS, ALL_CELLS), 1.0, 6.0, ((0, 16), (1, 32)))
    reports = scatter_about(arg_keys[1], (REGIONS, REPORTS), 1.0, 6.0, ((0, 32),), jnp.float32)
    report_count = draw_report_count(jax.random.fold_in(arg_keys[6], 71), 0)
    report_cell = draw_report_cell(jax.random.fold_in(arg_keys[6], 71), 0)
    report_weight = jnp.clip(jnp.exp(math.log(1.0) - 6.9077552 * jax.random.uniform(arg_keys[4], (REGIONS, POINTS, REPORTS), jnp.float32) ** block_levels(arg_keys[4], (REGIONS, POINTS, REPORTS), ((0, 32), (1, 16)), -0.2, 0.2)), 0.001, 1.0)
    blending = jnp.clip(jnp.exp(math.log(1.0) - 3.912023 * jax.random.uniform(arg_keys[5], (4, ALL_CELLS), jnp.float32) ** block_levels(arg_keys[5], (4, ALL_CELLS), ((1, 512),), -0.2, 0.2)), 0.02, 1.0)
    return dict(ensemble=ensemble, reports=reports, report_count=report_count, report_cell=report_cell, report_weight=report_weight, blending=blending)


highest = lax.Precision.HIGHEST

def make_transform(products, forcing, members):
    identity = jnp.eye(members, dtype=jnp.float32)
    precision_mat = (members - 1.0) * identity[None] + products
    frobenius = jnp.sqrt(lax.optimization_barrier(jnp.sum(precision_mat * precision_mat, axis=(1, 2))))
    current = precision_mat / frobenius[:, None, None]
    root_iter = jnp.broadcast_to(identity, current.shape)
    for iteration in range(SWEEPS):
        middle = 1.5 * identity[None] - 0.5 * jnp.einsum('aij,ajk->aik', root_iter, current, precision=highest)
        current = jnp.einsum('aij,ajk->aik', current, middle, precision=highest)
        root_iter = jnp.einsum('aij,ajk->aik', middle, root_iter, precision=highest)
    inverse_root = root_iter / jnp.sqrt(frobenius)[:, None, None]
    inner_step = jnp.einsum('aij,aj->ai', inverse_root, forcing, precision=highest)
    mean_weights = jnp.einsum('aij,aj->ai', inverse_root, inner_step, precision=highest)
    return (mean_weights[:, :, None] + jnp.sqrt(members - 1.0) * inverse_root).astype(jnp.bfloat16)

def corner_layout(band_index, points_here, row_count):
    group_index = jnp.arange(4 * points_here, dtype=jnp.int32)
    upper_half = group_index // (2 * points_here)
    column_block = group_index // 2 % points_here
    right_half = group_index % 2
    row_base = jnp.clip(band_index - 1 + upper_half, 0, row_count - 2)
    col_base = jnp.clip(column_block - 1 + right_half, 0, points_here - 2)
    return (row_base, col_base)

def reference(ensemble, reports, report_count, report_cell, report_weight, blending):
    members = ensemble.shape[0]
    regions = reports.shape[0]
    cell_count = ensemble.shape[1] // regions
    groups_band = 4 * POINTS_DEV
    group_cells = cell_count // (POINT_ROWS * groups_band)
    mixing_all = blending / lax.optimization_barrier(jnp.sum(blending, axis=0, keepdims=True))
    bands = jnp.arange(POINT_ROWS, dtype=jnp.int32)[:, None]
    row_base, col_base = corner_layout(bands, POINTS_DEV, POINT_ROWS)

    def per_region(region):
        at_reports = jnp.take(ensemble, report_cell[region], axis=1).astype(jnp.float32)
        report_mean = lax.optimization_barrier(jnp.sum(at_reports, axis=0)) / members
        report_pert = (at_reports - report_mean[None, :]).astype(jnp.bfloat16)
        active = (jnp.arange(report_pert.shape[1]) < report_count[region]).astype(jnp.float32)
        weights = report_weight[region] * active[None, :]
        weighted = (report_pert.astype(jnp.float32)[None, :, :] * weights[:, None, :]).astype(jnp.bfloat16)
        departure = (weights * (reports[region] - report_mean)[None, :]).astype(jnp.bfloat16)
        products = jnp.einsum('ako,jo->akj', weighted.astype(jnp.float32), report_pert.astype(jnp.float32), precision=highest)
        forcing = jnp.einsum('ao,ko->ak', departure.astype(jnp.float32), report_pert.astype(jnp.float32), precision=highest)
        transform = make_transform(products, forcing, members)
        block_cells = lax.dynamic_slice_in_dim(ensemble, region * cell_count, cell_count, 1).astype(jnp.float32)
        cell_mean = lax.optimization_barrier(jnp.sum(block_cells, axis=0)) / members
        anomaly = (block_cells - cell_mean[None, :]).astype(jnp.bfloat16)
        anomaly_view = anomaly.astype(jnp.float32).reshape(members, POINT_ROWS, groups_band, group_cells)
        mixing = lax.dynamic_slice_in_dim(mixing_all, region * cell_count, cell_count, 1)
        mixing = mixing.reshape(4, POINT_ROWS, groups_band, group_cells)
        blended = jnp.zeros((POINT_ROWS, groups_band, group_cells, members), jnp.float32)
        for corner in range(4):
            row_step = corner // 2
            col_step = corner % 2
            chosen_index = ((row_base + row_step) * POINTS_DEV + col_base + col_step).reshape(-1)
            chosen = jnp.take(transform, chosen_index, axis=0).astype(jnp.float32)
            chosen = chosen.reshape(POINT_ROWS, groups_band, members, members)
            spread = jnp.einsum('kngc,ngkj->ngcj', anomaly_view, chosen, precision=highest)
            blended = blended + mixing[corner][..., None] * spread
        blended = blended.reshape(cell_count, members)
        return (cell_mean[:, None] + blended).astype(jnp.bfloat16)
    result = lax.map(per_region, jnp.arange(regions, dtype=jnp.int32))
    return result.reshape(regions * cell_count, members)
```

```python
import functools
import math

import jax
import jax.numpy as jnp
from jax import lax
from jax.experimental import pallas as pl
from jax.experimental.pallas import tpu as pltpu
from jax.sharding import PartitionSpec as P

MESH = pl.DeviceIdType.MESH
MARGIN = 128
F32 = jnp.float32
BF16 = jnp.bfloat16


def split(value):
    high = value.astype(BF16)
    low = (value - high.astype(F32)).astype(BF16)
    return high, low


def dot(a, b):
    return jnp.dot(a, b, preferred_element_type=F32)


def dot_nt(a, b):
    return lax.dot_general(a, b, (((1,), (1,)), ((), ())), preferred_element_type=F32)


def left(parts):
    high, low = parts
    return jnp.concatenate([high, high, low], axis=1)


def right(parts):
    high, low = parts
    return jnp.concatenate([high, low, high], axis=0)


def kernel(
    count_ref, ens_ref, rep_ref, cell_ref, rw_ref, bl_ref, out_ref,
    at_buf, cells_buf, extra_buf, bl_buf, bord, fwd, picked, sent, got, anom, extra_anom, mean_col,
    x_s, z_s, t_s, forcing_s,
    bz_send, bz_recv, by_send, by_recv, at_send, at_recv, ce_send, ce_recv, fw_send, fw_recv,
    bl_send, bl_recv, xs_send, xs_recv, cn_send, cn_recv,
):
    region = lax.axis_index("region")
    me = lax.axis_index("member")
    local, cells = ens_ref.shape
    n = 16
    members = n * local
    zs, ys = 4, 8
    y, z = region // zs, region % zs
    half = cells // n // 2
    slots = at_buf.shape[1]
    first = (n - 1 - me) // (n - 1)
    last = me // (n - 1)

    def peer(i):
        return lax.rem(me + i, n)

    def zpeer(i):
        return y * zs + lax.rem(z + i, zs)

    def ypeer(i):
        return lax.rem(y + i, ys) * zs + z

    def rows(d):
        return pl.ds(pl.multiple_of(d * local, local), local)

    def remote(src, dst, ss, rs, **where):
        return pltpu.make_async_remote_copy(
            src_ref=src, dst_ref=dst, send_sem=ss, recv_sem=rs, device_id=where, device_id_type=MESH
        )

    barrier = pltpu.get_barrier_semaphore()

    def greet(i, c):
        pl.semaphore_signal(barrier, inc=1, device_id={"member": peer(i)}, device_id_type=MESH)
        return c

    def greet_z(i, c):
        pl.semaphore_signal(barrier, inc=1, device_id={"region": zpeer(i)}, device_id_type=MESH)
        return c

    def greet_y(i, c):
        pl.semaphore_signal(barrier, inc=1, device_id={"region": ypeer(i)}, device_id_type=MESH)
        return c

    lax.fori_loop(1, zs, greet_z, 0)
    lax.fori_loop(1, ys, greet_y, 0)
    lax.fori_loop(1, n, greet, 0)
    pl.semaphore_wait(barrier, zs + ys + n - 3)

    def z_copy(i):
        return remote(ens_ref.at[:, pl.ds(0, MARGIN)], bord.at[region], bz_send.at[i], bz_recv.at[i], region=zpeer(i))

    def y_copy(i):
        block = bord.at[pl.ds(y * zs, zs)]
        return remote(block, block, by_send.at[i], by_recv.at[i], region=ypeer(i))

    def at_copy(i):
        block = at_buf.at[rows(me)]
        return remote(block, block, at_send.at[i], at_recv.at[i], member=peer(i))

    def cell_start(d):
        return pl.multiple_of(2 * half * d - half + half * ((n - 1 - d) // (n - 1)) - half * (d // (n - 1)), MARGIN)

    def ce_copy(i):
        source = ens_ref.at[:, pl.ds(cell_start(peer(i)), 4 * half)]
        return remote(source, cells_buf.at[rows(me)], ce_send.at[i], ce_recv.at[i], member=peer(i))

    def fw_copy(i):
        return remote(fwd, picked.at[rows(me)], fw_send.at[i], fw_recv.at[i], member=peer(i))

    def started(copy):
        def body(i, c):
            copy(i).start()
            return c
        return body

    def sent_off(copy):
        def body(i, c):
            copy(i).wait_send()
            return c
        return body

    def arrived(copy):
        def body(i, c):
            copy(i).wait_recv()
            return c
        return body

    lax.fori_loop(1, zs, started(z_copy), 0)
    bord[region] = ens_ref[:, pl.ds(0, MARGIN)]

    up = remote(bl_ref, bl_buf.at[0], bl_send.at[0], bl_recv.at[0], member=lax.rem(me + 1, n))
    down = remote(bl_ref, bl_buf.at[1], bl_send.at[1], bl_recv.at[1], member=lax.rem(me + n - 1, n))
    up.start()
    down.start()

    lax.fori_loop(1, zs, arrived(z_copy), 0)
    lax.fori_loop(1, ys, started(y_copy), 0)

    target = cell_ref[...]
    relative = target - region * cells
    is_local = (relative >= 0) & (relative < cells)
    lane = lax.rem(jnp.where(is_local, relative, 0), MARGIN)
    column = jnp.where(is_local, relative // MARGIN, -1)
    blocks = slots // MARGIN
    lanes = [jnp.broadcast_to(lane[:, b * MARGIN:(b + 1) * MARGIN], (local, MARGIN)) for b in range(blocks)]
    columns = [jnp.broadcast_to(column[:, b * MARGIN:(b + 1) * MARGIN], (local, MARGIN)) for b in range(blocks)]

    def gather(h, accs):
        chunk = ens_ref[:, pl.ds(pl.multiple_of(h * MARGIN, MARGIN), MARGIN)].astype(F32)
        return tuple(
            jnp.where(columns[b] == h, jnp.take_along_axis(chunk, lanes[b], axis=1, mode="promise_in_bounds"), accs[b])
            for b in range(blocks)
        )

    accs = lax.fori_loop(0, cells // MARGIN, gather, tuple(jnp.zeros((local, MARGIN), F32) for _ in range(blocks)))
    at_buf[rows(me), :] = jnp.concatenate(accs, axis=1).astype(BF16)
    lax.fori_loop(1, n, started(at_copy), 0)

    holder = (target // cells).astype(F32)
    s_low = jnp.min(jnp.where(is_local, 1e6, holder), axis=1, keepdims=True)
    s_high = jnp.max(jnp.where(is_local, -1.0, holder), axis=1, keepdims=True)
    lax.fori_loop(1, ys, arrived(y_copy), 0)

    def pick(s, c):
        low, high = c
        block = bord[s].astype(F32)
        at = s.astype(F32)
        return jnp.where(s_low == at, block, low), jnp.where(s_high == at, block, high)

    nothing = jnp.zeros((local, MARGIN), F32)
    low, high = lax.fori_loop(0, zs * ys, pick, (nothing, nothing))
    mine = jnp.concatenate([low, high], axis=1).astype(BF16)
    fwd[...] = mine
    picked[rows(me), :] = mine
    lax.fori_loop(1, n, started(fw_copy), 0)

    lax.fori_loop(1, n, started(ce_copy), 0)
    cells_buf[rows(me), :] = ens_ref[:, pl.ds(cell_start(me), 4 * half)]

    def extra_copy(k):
        d = (1, n - 2)[k]
        source = ens_ref.at[:, pl.ds((0, cells - half)[k], half)]
        return remote(source, extra_buf.at[rows(me)], xs_send.at[k], xs_recv.at[me], member=d)

    for k, d in enumerate((1, n - 2)):
        @pl.when(me != d)
        def _():
            extra_copy(k).start()

        @pl.when(me == d)
        def _():
            extra_buf[rows(me), :] = ens_ref[:, pl.ds((0, cells - half)[k], half)]

    lax.fori_loop(1, n, arrived(fw_copy), 0)
    lax.fori_loop(1, n, arrived(at_copy), 0)
    within = lax.rem(target, cells)
    key = jnp.where(
        is_local, -1,
        jnp.where(holder == s_low, within, jnp.where(holder == s_high, MARGIN + within, -1)),
    )
    onehot = (lax.broadcasted_iota(jnp.int32, (2 * MARGIN, slots), 0) == key).astype(F32).astype(BF16)
    at_reports = at_buf[...].astype(F32) + dot(picked[...], onehot)
    mean = jnp.sum(at_reports, axis=0, keepdims=True) * (1.0 / members)
    pert = (at_reports - mean).astype(BF16)
    pert_wide = pert.astype(F32)
    active = lax.broadcasted_iota(jnp.int32, (1, slots), 1) < count_ref[0]
    weights = jnp.where(active, rw_ref[...], 0.0)
    points = weights.shape[0]
    departure = weights * (rep_ref[...] - mean)
    departure = jnp.concatenate([departure, jnp.zeros((MARGIN - points, slots), F32)], axis=0).astype(BF16)
    forcing_s[...] = dot_nt(pert, departure)
    eye = (
        lax.broadcasted_iota(jnp.int32, (members, members), 0)
        == lax.broadcasted_iota(jnp.int32, (members, members), 1)
    ).astype(F32)
    frob = []
    for q in range(points):
        weighted = (pert_wide * weights[q:q + 1]).astype(BF16)
        precision_mat = (members - 1.0) * eye + dot_nt(weighted, pert)
        squares = jnp.sum(jnp.sum(precision_mat * precision_mat, axis=0, keepdims=True), axis=1, keepdims=True)
        f = jnp.sqrt(squares)
        frob.append(f)
        a = precision_mat * (1.0 / f)
        middle = 1.5 * eye - 0.5 * a
        m = right(split(middle))
        inner = dot(left(split(a)), m)
        x_s[q] = dot(left(split(inner)), m)
        z_s[q] = middle

    def sweep(i, c):
        for q in range(points):
            x = x_s[q]
            m = right(split(1.5 * eye - 0.5 * x))
            inner = dot(left(split(x)), m)
            z_s[q] = dot(left(split(z_s[q])), m)
            x_s[q] = dot(left(split(inner)), m)
        return c

    lax.fori_loop(0, 2, sweep, 0)
    for q in range(points):
        m = right(split(1.5 * eye - 0.5 * x_s[q]))
        root = dot(left(split(z_s[q])), m)
        root_parts = left(split(root))
        step = dot(root_parts, right(split(forcing_s[...])))
        mean_weights = dot(root_parts, right(split(step))) * (1.0 / frob[q])
        t_s[q] = (mean_weights[:, q:q + 1] + (math.sqrt(members - 1.0) * lax.rsqrt(frob[q])) * root).astype(BF16)

    lax.fori_loop(1, n, arrived(ce_copy), 0)

    def turn(values):
        across = values.astype(F32).T
        mean = jnp.sum(across, axis=1, keepdims=True) * (1.0 / members)
        return mean, (across - mean).astype(BF16)

    for b in range(4):
        cut = slice(b * half, (b + 1) * half)
        mean_col[cut], anom[cut] = turn(cells_buf[:, cut])

    up.wait_recv()
    down.wait_recv()

    def mixed(values):
        return values * (1.0 / jnp.sum(values, axis=0, keepdims=True))

    own, below, above = mixed(bl_ref[...]), mixed(bl_buf[0]), mixed(bl_buf[1])
    weights_of = [
        below[2:4, half:],
        jnp.where(me == 0, own[0:2, :half], own[2:4, :half]),
        jnp.where(me == n - 1, own[2:4, half:], own[0:2, half:]),
        above[0:2, :half],
        jnp.where(me == 1, below[2:4, :half], above[0:2, half:]),
    ]
    stacked = jnp.concatenate(weights_of + [jnp.zeros((MARGIN - 10, half), F32)], axis=0)
    mix = stacked.T

    narrow, wide = 3 * half // 8, 5 * half // 8

    def blended(values, b):
        w0, w1 = mix[:, 2 * b:2 * b + 1], mix[:, 2 * b + 1:2 * b + 2]
        s0 = dot(values[:narrow], t_s[0])
        s1 = dot(values[:wide], t_s[1])
        s2 = dot(values[narrow:], t_s[2])
        s3 = dot(values[wide:], t_s[3])
        return jnp.concatenate([
            w0[:narrow] * s0 + w1[:narrow] * s1[:narrow],
            w0[narrow:wide] * s1[narrow:] + w1[narrow:wide] * s2[:wide - narrow],
            w0[wide:] * s2[wide - narrow:] + w1[wide:] * s3,
        ], axis=0)

    base = pl.multiple_of(half * (1 - first + last), half)

    def part(offset):
        return pl.ds(pl.multiple_of(base + offset, half), half)

    def out_copy(k, d, side):
        return remote(sent.at[k], got.at[side], cn_send.at[k], cn_recv.at[side], member=d)

    @pl.when(me < n - 1)
    def _():
        sent[0] = blended(anom[part(2 * half)], 3).astype(BF16)
        out_copy(0, me + 1, 0).start()

    @pl.when(me > 0)
    def _():
        sent[1] = blended(anom[part(-half)], 0).astype(BF16)
        out_copy(1, me - 1, 1).start()

    for k, d, target_d, side in ((0, 1, 0, 0), (1, n - 2, n - 1, 1)):
        @pl.when(me == d)
        def _():
            def extra_in(i, c):
                src = peer(i)
                remote(
                    ens_ref.at[:, pl.ds(0, half)], extra_buf.at[rows(src)], xs_send.at[k], xs_recv.at[src], member=src
                ).wait_recv()
                return c

            lax.fori_loop(1, n, extra_in, 0)
            sent[2] = blended(turn(extra_buf[...])[1], 4).astype(BF16)
            out_copy(2, target_d, side).start()

    mine_0 = mean_col[part(0)] + blended(anom[part(0)], 1)
    mine_1 = mean_col[part(half)] + blended(anom[part(half)], 2)
    out_copy(0, lax.rem(me + 1, n), 0).wait_recv()
    out_ref[:half] = (mine_0 + got[0].astype(F32)).astype(BF16)
    out_copy(1, lax.rem(me + n - 1, n), 1).wait_recv()
    out_ref[half:] = (mine_1 + got[1].astype(F32)).astype(BF16)

    lax.fori_loop(1, zs, sent_off(z_copy), 0)
    lax.fori_loop(1, ys, sent_off(y_copy), 0)
    lax.fori_loop(1, n, sent_off(at_copy), 0)
    lax.fori_loop(1, n, sent_off(fw_copy), 0)
    lax.fori_loop(1, n, sent_off(ce_copy), 0)
    up.wait_send()
    down.wait_send()
    for k, d in enumerate((1, n - 2)):
        @pl.when(me != d)
        def _():
            extra_copy(k).wait_send()

        @pl.when(me == d)
        def _():
            out_copy(2, 0, 0).wait_send()

    @pl.when(me < n - 1)
    def _():
        out_copy(0, me + 1, 0).wait_send()

    @pl.when(me > 0)
    def _():
        out_copy(1, me - 1, 1).wait_send()


def per_device(ensemble, reports, report_count, report_cell, report_weight, blending):
    local, cells = ensemble.shape
    n = lax.axis_size("member")
    members = n * local
    slots = reports.shape[1]
    points = report_weight.shape[1]
    half = cells // n // 2
    vmem = pl.BlockSpec(memory_space=pltpu.VMEM)
    dma = pltpu.SemaphoreType.DMA
    return pl.pallas_call(
        kernel,
        out_shape=jax.ShapeDtypeStruct((cells // n, members), BF16),
        in_specs=[pl.BlockSpec(memory_space=pltpu.SMEM)] + [vmem] * 5,
        out_specs=vmem,
        scratch_shapes=[
            pltpu.VMEM((members, slots), BF16),
            pltpu.VMEM((members, 4 * half), BF16),
            pltpu.VMEM((members, half), BF16),
            pltpu.VMEM((2, 4, 2 * half), F32),
            pltpu.VMEM((lax.axis_size("region"), local, MARGIN), BF16),
            pltpu.VMEM((local, 2 * MARGIN), BF16),
            pltpu.VMEM((members, 2 * MARGIN), BF16),
            pltpu.VMEM((3, half, members), BF16),
            pltpu.VMEM((2, half, members), BF16),
            pltpu.VMEM((4 * half, members), BF16),
            pltpu.VMEM((half, members), BF16),
            pltpu.VMEM((4 * half, 1), F32),
            pltpu.VMEM((points, members, members), F32),
            pltpu.VMEM((points, members, members), F32),
            pltpu.VMEM((points, members, members), BF16),
            pltpu.VMEM((members, MARGIN), F32),
            dma((4,)), dma((4,)), dma((8,)), dma((8,)), dma((n,)), dma((n,)), dma((n,)), dma((n,)), dma((n,)), dma((n,)),
            dma((2,)), dma((2,)), dma((2,)), dma((n,)), dma((3,)), dma((2,)),
        ],
        compiler_params=pltpu.CompilerParams(
            collective_id=0, has_side_effects=True, vmem_limit_bytes=48 * 1024 * 1024
        ),
    )(report_count, ensemble, reports, report_cell, report_weight[0], blending)


def solution(mesh):
    return jax.shard_map(
        per_device,
        mesh=mesh,
        in_specs=(
            P("member", "region"),
            P("region", None),
            P("region"),
            P("region", None),
            P("region", "member", None),
            P(None, ("region", "member")),
        ),
        out_specs=P(("region", "member"), None),
        check_vma=False,
    )
```

```python
import functools
import math

import jax
import jax.numpy as jnp
from jax import lax
from jax.experimental import pallas as pl
from jax.experimental.pallas import tpu as pltpu
from jax.sharding import PartitionSpec as P

MESH = pl.DeviceIdType.MESH
MARGIN = 128
F32 = jnp.float32
BF16 = jnp.bfloat16


def split(value):
    high = value.astype(BF16)
    low = (value - high.astype(F32)).astype(BF16)
    return high, low


def dot(a, b):
    return jnp.dot(a, b, preferred_element_type=F32)


def dot_nt(a, b):
    return lax.dot_general(a, b, (((1,), (1,)), ((), ())), preferred_element_type=F32)


def dot_tn(a, b):
    return lax.dot_general(a, b, (((0,), (0,)), ((), ())), preferred_element_type=F32)


def left(parts):
    high, low = parts
    return jnp.concatenate([high, high, low], axis=1)


def right(parts):
    high, low = parts
    return jnp.concatenate([high, low, high], axis=0)


def kernel(
    count_hbm, ens_hbm, rep_hbm, cell_hbm, rw_hbm, bl_hbm, out_ref,
    count_ref, ens_ref, rep_ref, cell_ref, rw_ref, bl_ref, in_sem,
    at_buf, cells_buf, extra_buf, bl_buf, bord, fwd, picked, sent, got, anom, extra_anom, mean_col,
    wide_ens, x_s, z_s, t_s, forcing_s,
    bo_send, bo_recv, at_send, at_recv, ce_send, ce_recv, fw_send, fw_recv,
    bl_send, bl_recv, xs_send, xs_recv, cn_send, cn_recv,
):
    loads = [
        pltpu.make_async_copy(source, landed, in_sem.at[i])
        for i, (source, landed) in enumerate((
            (cell_hbm, cell_ref), (ens_hbm, ens_ref), (bl_hbm, bl_ref), (rw_hbm, rw_ref), (rep_hbm, rep_ref), (count_hbm, count_ref)
        ))
    ]
    for load in loads:
        load.start()
    region = lax.axis_index("region")
    me = lax.axis_index("member")
    local, cells = ens_ref.shape
    n = 16
    members = n * local
    regions = bord.shape[0]
    half = cells // n // 2
    slots = at_buf.shape[1]
    first = (n - 1 - me) // (n - 1)
    last = me // (n - 1)

    def peer(i):
        return lax.rem(me + i, n)

    def region_peer(i):
        return lax.rem(region + i, regions)

    def rows(d):
        return pl.ds(pl.multiple_of(d * local, local), local)

    def remote(src, dst, ss, rs, **where):
        return pltpu.make_async_remote_copy(
            src_ref=src, dst_ref=dst, send_sem=ss, recv_sem=rs, device_id=where, device_id_type=MESH
        )

    barrier = pltpu.get_barrier_semaphore()

    def greet(i, c):
        pl.semaphore_signal(barrier, inc=1, device_id={"member": peer(i)}, device_id_type=MESH)
        return c

    def greet_region(i, c):
        pl.semaphore_signal(barrier, inc=1, device_id={"region": region_peer(i)}, device_id_type=MESH)
        return c

    lax.fori_loop(1, regions, greet_region, 0)
    lax.fori_loop(1, n, greet, 0)
    for load in loads:
        load.wait()

    def border_copy(i):
        source = ens_ref.at[:, pl.ds(0, MARGIN)]
        return remote(source, bord.at[region], bo_send.at[i], bo_recv.at[i], region=region_peer(i))

    def at_copy(i):
        block = at_buf.at[rows(me)]
        return remote(block, block, at_send.at[i], at_recv.at[i], member=peer(i))

    def cell_start(d):
        return pl.multiple_of(2 * half * d - half + half * ((n - 1 - d) // (n - 1)) - half * (d // (n - 1)), MARGIN)

    def ce_copy(i):
        source = ens_ref.at[:, pl.ds(cell_start(peer(i)), 4 * half)]
        return remote(source, cells_buf.at[rows(me)], ce_send.at[i], ce_recv.at[i], member=peer(i))

    def fw_copy(i):
        return remote(fwd, picked.at[rows(me)], fw_send.at[i], fw_recv.at[i], member=peer(i))

    def started(copy):
        def body(i, c):
            copy(i).start()
            return c
        return body

    def sent_off(copy):
        def body(i, c):
            copy(i).wait_send()
            return c
        return body

    def arrived(copy):
        def body(i, c):
            copy(i).wait_recv()
            return c
        return body

    target = cell_ref[...]
    relative = target - region * cells
    is_local = (relative >= 0) & (relative < cells)
    lane = lax.rem(jnp.where(is_local, relative, 0), MARGIN)
    column = jnp.where(is_local, relative // MARGIN, -1)
    for h in range(cells // MARGIN):
        wide_ens[h * local:(h + 1) * local, :] = ens_ref[:, h * MARGIN:(h + 1) * MARGIN].astype(F32)
    in_column = (lax.broadcasted_iota(jnp.int32, (cells // MARGIN, slots), 0) == column).astype(F32).astype(BF16)
    in_lane = lax.broadcasted_iota(jnp.int32, (MARGIN, slots), 0) == lane
    gathered = []
    for k in range(local):
        values = wide_ens[pl.ds(k, cells // MARGIN, stride=local), :].astype(BF16)
        found = dot_tn(values, in_column)
        gathered.append(jnp.sum(jnp.where(in_lane, found, 0.0), axis=0, keepdims=True))
    at_buf[rows(me), :] = jnp.concatenate(gathered, axis=0).astype(BF16)
    bord[region] = ens_ref[:, pl.ds(0, MARGIN)]

    pl.semaphore_wait(barrier, regions + n - 2)
    up = remote(bl_ref, bl_buf.at[0], bl_send.at[0], bl_recv.at[0], member=lax.rem(me + 1, n))
    down = remote(bl_ref, bl_buf.at[1], bl_send.at[1], bl_recv.at[1], member=lax.rem(me + n - 1, n))
    lax.fori_loop(1, regions, started(border_copy), 0)
    lax.fori_loop(1, n, started(at_copy), 0)
    up.start()
    down.start()

    holder = (target // cells).astype(F32)
    s_low = jnp.min(jnp.where(is_local, 1e6, holder), axis=1, keepdims=True)
    s_high = jnp.max(jnp.where(is_local, -1.0, holder), axis=1, keepdims=True)
    lax.fori_loop(1, regions, arrived(border_copy), 0)

    def pick(s, c):
        low, high = c
        block = bord[s].astype(F32)
        at = s.astype(F32)
        return jnp.where(s_low == at, block, low), jnp.where(s_high == at, block, high)

    nothing = jnp.zeros((local, MARGIN), F32)
    low, high = lax.fori_loop(0, regions, pick, (nothing, nothing), unroll=8)
    mine = jnp.concatenate([low, high], axis=1).astype(BF16)
    fwd[...] = mine
    picked[rows(me), :] = mine
    lax.fori_loop(1, n, started(fw_copy), 0)

    lax.fori_loop(1, n, started(ce_copy), 0)
    cells_buf[rows(me), :] = ens_ref[:, pl.ds(cell_start(me), 4 * half)]

    def extra_copy(k):
        d = (1, n - 2)[k]
        source = ens_ref.at[:, pl.ds((0, cells - half)[k], half)]
        return remote(source, extra_buf.at[rows(me)], xs_send.at[k], xs_recv.at[me], member=d)

    for k, d in enumerate((1, n - 2)):
        @pl.when(me != d)
        def _():
            extra_copy(k).start()

        @pl.when(me == d)
        def _():
            extra_buf[rows(me), :] = ens_ref[:, pl.ds((0, cells - half)[k], half)]

    lax.fori_loop(1, n, arrived(fw_copy), 0)
    lax.fori_loop(1, n, arrived(at_copy), 0)
    within = lax.rem(target, cells)
    key = jnp.where(
        is_local, -1,
        jnp.where(holder == s_low, within, jnp.where(holder == s_high, MARGIN + within, -1)),
    )
    onehot = (lax.broadcasted_iota(jnp.int32, (2 * MARGIN, slots), 0) == key).astype(F32).astype(BF16)
    at_reports = at_buf[...].astype(F32) + dot(picked[...], onehot)
    mean = jnp.sum(at_reports, axis=0, keepdims=True) * (1.0 / members)
    pert = (at_reports - mean).astype(BF16)
    pert_wide = pert.astype(F32)
    active = lax.broadcasted_iota(jnp.int32, (1, slots), 1) < count_ref[0]
    weights = jnp.where(active, rw_ref[...], 0.0)
    points = weights.shape[0]
    departure = weights * (rep_ref[...] - mean)
    departure = jnp.concatenate([departure, jnp.zeros((MARGIN - points, slots), F32)], axis=0).astype(BF16)
    forcing_s[...] = dot_nt(pert, departure)
    eye = (
        lax.broadcasted_iota(jnp.int32, (members, members), 0)
        == lax.broadcasted_iota(jnp.int32, (members, members), 1)
    ).astype(F32)
    frob = []
    for q in range(points):
        weighted = (pert_wide * weights[q:q + 1]).astype(BF16)
        precision_mat = (members - 1.0) * eye + dot_nt(weighted, pert)
        squares = jnp.sum(jnp.sum(precision_mat * precision_mat, axis=0, keepdims=True), axis=1, keepdims=True)
        f = jnp.sqrt(squares)
        frob.append(f)
        a = precision_mat * (1.0 / f)
        middle = 1.5 * eye - 0.5 * a
        m = right(split(middle))
        inner = dot(left(split(a)), m)
        x_s[q] = dot(left(split(inner)), m)
        z_s[q] = middle

    def sweep(i, c):
        for q in range(points):
            x = x_s[q]
            m = right(split(1.5 * eye - 0.5 * x))
            inner = dot(left(split(x)), m)
            z_s[q] = dot(left(split(z_s[q])), m)
            x_s[q] = dot(left(split(inner)), m)
        return c

    lax.fori_loop(0, 2, sweep, 0)
    for q in range(points):
        m = right(split(1.5 * eye - 0.5 * x_s[q]))
        root = dot(left(split(z_s[q])), m)
        step = jnp.sum(root * forcing_s[:, q:q + 1], axis=0, keepdims=True)
        mean_weights = jnp.sum(root * step, axis=1, keepdims=True) * (1.0 / frob[q])
        t_s[q] = (mean_weights + (math.sqrt(members - 1.0) * lax.rsqrt(frob[q])) * root).astype(BF16)

    lax.fori_loop(1, n, arrived(ce_copy), 0)

    def turn(values):
        across = values.astype(F32).T
        mean = jnp.sum(across, axis=1, keepdims=True) * (1.0 / members)
        return mean, (across - mean).astype(BF16)

    for b in range(4):
        cut = slice(b * half, (b + 1) * half)
        mean_col[cut], anom[cut] = turn(cells_buf[:, cut])

    up.wait_recv()
    down.wait_recv()

    def mixed(values):
        return values * (1.0 / jnp.sum(values, axis=0, keepdims=True))

    own, below, above = mixed(bl_ref[...]), mixed(bl_buf[0]), mixed(bl_buf[1])
    weights_of = [
        below[2:4, half:],
        jnp.where(me == 0, own[0:2, :half], own[2:4, :half]),
        jnp.where(me == n - 1, own[2:4, half:], own[0:2, half:]),
        above[0:2, :half],
        jnp.where(me == 1, below[2:4, :half], above[0:2, half:]),
    ]
    stacked = jnp.concatenate(weights_of + [jnp.zeros((MARGIN - 10, half), F32)], axis=0)
    mix = stacked.T

    narrow, wide = 3 * half // 8, 5 * half // 8

    def blended(values, b):
        w0, w1 = mix[:, 2 * b:2 * b + 1], mix[:, 2 * b + 1:2 * b + 2]
        s0 = dot(values[:narrow], t_s[0])
        s1 = dot(values[:wide], t_s[1])
        s2 = dot(values[narrow:], t_s[2])
        s3 = dot(values[wide:], t_s[3])
        return jnp.concatenate([
            w0[:narrow] * s0 + w1[:narrow] * s1[:narrow],
            w0[narrow:wide] * s1[narrow:] + w1[narrow:wide] * s2[:wide - narrow],
            w0[wide:] * s2[wide - narrow:] + w1[wide:] * s3,
        ], axis=0)

    base = pl.multiple_of(half * (1 - first + last), half)

    def part(offset):
        return pl.ds(pl.multiple_of(base + offset, half), half)

    def out_copy(k, d, side):
        return remote(sent.at[k], got.at[side], cn_send.at[k], cn_recv.at[side], member=d)

    @pl.when(me < n - 1)
    def _():
        sent[0] = blended(anom[part(2 * half)], 3).astype(BF16)
        out_copy(0, me + 1, 0).start()

    @pl.when(me > 0)
    def _():
        sent[1] = blended(anom[part(-half)], 0).astype(BF16)
        out_copy(1, me - 1, 1).start()

    for k, d, target_d, side in ((0, 1, 0, 0), (1, n - 2, n - 1, 1)):
        @pl.when(me == d)
        def _():
            def extra_in(i, c):
                src = peer(i)
                remote(
                    ens_ref.at[:, pl.ds(0, half)], extra_buf.at[rows(src)], xs_send.at[k], xs_recv.at[src], member=src
                ).wait_recv()
                return c

            lax.fori_loop(1, n, extra_in, 0)
            sent[2] = blended(turn(extra_buf[...])[1], 4).astype(BF16)
            out_copy(2, target_d, side).start()

    mine_0 = mean_col[part(0)] + blended(anom[part(0)], 1)
    mine_1 = mean_col[part(half)] + blended(anom[part(half)], 2)
    lax.fori_loop(1, regions, sent_off(border_copy), 0)
    lax.fori_loop(1, n, sent_off(at_copy), 0)
    lax.fori_loop(1, n, sent_off(fw_copy), 0)
    lax.fori_loop(1, n, sent_off(ce_copy), 0)
    up.wait_send()
    down.wait_send()
    for k, d in enumerate((1, n - 2)):
        @pl.when(me != d)
        def _():
            extra_copy(k).wait_send()

        @pl.when(me == d)
        def _():
            out_copy(2, 0, 0).wait_send()

    @pl.when(me < n - 1)
    def _():
        out_copy(0, me + 1, 0).wait_send()

    @pl.when(me > 0)
    def _():
        out_copy(1, me - 1, 1).wait_send()

    out_copy(0, lax.rem(me + 1, n), 0).wait_recv()
    out_ref[:half] = (mine_0 + got[0].astype(F32)).astype(BF16)
    out_copy(1, lax.rem(me + n - 1, n), 1).wait_recv()
    out_ref[half:] = (mine_1 + got[1].astype(F32)).astype(BF16)


def per_device(ensemble, reports, report_count, report_cell, report_weight, blending):
    local, cells = ensemble.shape
    n = lax.axis_size("member")
    members = n * local
    slots = reports.shape[1]
    points = report_weight.shape[1]
    half = cells // n // 2
    vmem = pl.BlockSpec(memory_space=pltpu.VMEM)
    anywhere = pl.BlockSpec(memory_space=pltpu.HBM)
    dma = pltpu.SemaphoreType.DMA
    return pl.pallas_call(
        kernel,
        out_shape=jax.ShapeDtypeStruct((cells // n, members), BF16),
        in_specs=[anywhere] * 6,
        out_specs=vmem,
        scratch_shapes=[
            pltpu.SMEM((1,), jnp.int32),
            pltpu.VMEM((local, cells), BF16),
            pltpu.VMEM((1, slots), F32),
            pltpu.VMEM((1, slots), jnp.int32),
            pltpu.VMEM((points, slots), F32),
            pltpu.VMEM((4, 2 * half), F32),
            dma((6,)),
            pltpu.VMEM((members, slots), BF16),
            pltpu.VMEM((members, 4 * half), BF16),
            pltpu.VMEM((members, half), BF16),
            pltpu.VMEM((2, 4, 2 * half), F32),
            pltpu.VMEM((lax.axis_size("region"), local, MARGIN), BF16),
            pltpu.VMEM((local, 2 * MARGIN), BF16),
            pltpu.VMEM((members, 2 * MARGIN), BF16),
            pltpu.VMEM((3, half, members), BF16),
            pltpu.VMEM((2, half, members), BF16),
            pltpu.VMEM((4 * half, members), BF16),
            pltpu.VMEM((half, members), BF16),
            pltpu.VMEM((4 * half, 1), F32),
            pltpu.VMEM((local * cells // MARGIN, MARGIN), F32),
            pltpu.VMEM((points, members, members), F32),
            pltpu.VMEM((points, members, members), F32),
            pltpu.VMEM((points, members, members), BF16),
            pltpu.VMEM((members, MARGIN), F32),
            dma((lax.axis_size("region"),)), dma((lax.axis_size("region"),)), dma((n,)), dma((n,)), dma((n,)), dma((n,)), dma((n,)), dma((n,)),
            dma((2,)), dma((2,)), dma((2,)), dma((n,)), dma((3,)), dma((2,)),
        ],
        compiler_params=pltpu.CompilerParams(
            collective_id=0, has_side_effects=True, vmem_limit_bytes=64 * 1024 * 1024
        ),
    )(report_count, ensemble, reports, report_cell, report_weight[0], blending)


def solution(mesh):
    return jax.shard_map(
        per_device,
        mesh=mesh,
        in_specs=(
            P("member", "region"),
            P("region", None),
            P("region"),
            P("region", None),
            P("region", "member", None),
            P(None, ("region", "member")),
        ),
        out_specs=P(("region", "member"), None),
        check_vma=False,
    )
```

```python
import functools
import math

import jax
import jax.numpy as jnp
from jax import lax
from jax.experimental import pallas as pl
from jax.experimental.pallas import tpu as pltpu
from jax.sharding import PartitionSpec as P

MESH = pl.DeviceIdType.MESH
MARGIN = 128
Z_CHIPS = 4
F32 = jnp.float32
BF16 = jnp.bfloat16


def split(value):
    high = value.astype(BF16)
    low = (value - high.astype(F32)).astype(BF16)
    return high, low


def dot(a, b):
    return jnp.dot(a, b, preferred_element_type=F32)


def dot_nt(a, b):
    return lax.dot_general(a, b, (((1,), (1,)), ((), ())), preferred_element_type=F32)


def dot_tn(a, b):
    return lax.dot_general(a, b, (((0,), (0,)), ((), ())), preferred_element_type=F32)


def kernel(
    count_hbm, ens_hbm, rep_hbm, cell_hbm, rw_hbm, bl_hbm, out_ref,
    count_ref, ens_ref, rep_ref, cell_ref, rw_ref, bl_ref, in_sem,
    at_buf, cells_buf, extra_buf, bl_buf, bord, fwd, picked, sent, got, anom, extra_anom, mean_col,
    wide_ens, x_s, z_s, t_s, forcing_s,
    bz_send, bz_recv, by_send, by_recv, at_send, at_recv, ce_send, ce_recv, fw_send, fw_recv,
    bl_send, bl_recv, xs_send, xs_recv, cn_send, cn_recv,
):
    loads = [
        pltpu.make_async_copy(source, landed, in_sem.at[i])
        for i, (source, landed) in enumerate((
            (cell_hbm, cell_ref), (ens_hbm, ens_ref), (bl_hbm, bl_ref), (rw_hbm, rw_ref), (rep_hbm, rep_ref), (count_hbm, count_ref)
        ))
    ]
    for load in loads:
        load.start()
    region = lax.axis_index("region")
    me = lax.axis_index("member")
    local, cells = ens_ref.shape
    zs = Z_CHIPS
    n = 16
    members = n * local
    regions = bord.shape[0]
    ys = regions // zs
    y, z = region // zs, region % zs
    half = cells // n // 2
    slots = at_buf.shape[1]
    first = (n - 1 - me) // (n - 1)
    last = me // (n - 1)

    def peer(i):
        return lax.rem(me + i, n)

    def z_peer(i):
        return y * zs + lax.rem(z + i, zs)

    def y_peer(i):
        return lax.rem(y + i, ys) * zs + z

    def rows(d):
        return pl.ds(pl.multiple_of(d * local, local), local)

    def remote(src, dst, ss, rs, **where):
        return pltpu.make_async_remote_copy(
            src_ref=src, dst_ref=dst, send_sem=ss, recv_sem=rs, device_id=where, device_id_type=MESH
        )

    barrier = pltpu.get_barrier_semaphore()

    def greet(i, c):
        pl.semaphore_signal(barrier, inc=1, device_id={"member": peer(i)}, device_id_type=MESH)
        return c

    def greet_z(i, c):
        pl.semaphore_signal(barrier, inc=1, device_id={"region": z_peer(i)}, device_id_type=MESH)
        return c

    def greet_y(i, c):
        pl.semaphore_signal(barrier, inc=1, device_id={"region": y_peer(i)}, device_id_type=MESH)
        return c

    lax.fori_loop(1, zs, greet_z, 0)
    lax.fori_loop(1, ys, greet_y, 0)
    lax.fori_loop(1, n, greet, 0)
    for load in loads:
        load.wait()

    def z_copy(i):
        source = ens_ref.at[:, pl.ds(0, MARGIN)]
        return remote(source, bord.at[region], bz_send.at[i], bz_recv.at[i], region=z_peer(i))

    def y_copy(i):
        block = bord.at[pl.ds(y * zs, zs)]
        return remote(block, block, by_send.at[i], by_recv.at[i], region=y_peer(i))

    def at_copy(i):
        block = at_buf.at[rows(me)]
        return remote(block, block, at_send.at[i], at_recv.at[i], member=peer(i))

    def cell_start(d):
        return pl.multiple_of(2 * half * d - half + half * ((n - 1 - d) // (n - 1)) - half * (d // (n - 1)), MARGIN)

    def ce_copy(i):
        source = ens_ref.at[:, pl.ds(cell_start(peer(i)), 4 * half)]
        return remote(source, cells_buf.at[rows(me)], ce_send.at[i], ce_recv.at[i], member=peer(i))

    def fw_copy(i):
        return remote(fwd, picked.at[rows(me)], fw_send.at[i], fw_recv.at[i], member=peer(i))

    def started(copy):
        def body(i, c):
            copy(i).start()
            return c
        return body

    def sent_off(copy):
        def body(i, c):
            copy(i).wait_send()
            return c
        return body

    def arrived(copy):
        def body(i, c):
            copy(i).wait_recv()
            return c
        return body

    target = cell_ref[...]
    relative = target - region * cells
    is_local = (relative >= 0) & (relative < cells)
    lane = lax.rem(jnp.where(is_local, relative, 0), MARGIN)
    column = jnp.where(is_local, relative // MARGIN, -1)
    for h in range(cells // MARGIN):
        wide_ens[h * local:(h + 1) * local, :] = ens_ref[:, h * MARGIN:(h + 1) * MARGIN].astype(F32)
    in_column = (lax.broadcasted_iota(jnp.int32, (cells // MARGIN, slots), 0) == column).astype(F32).astype(BF16)
    in_lane = lax.broadcasted_iota(jnp.int32, (MARGIN, slots), 0) == lane
    gathered = []
    for k in range(local):
        values = wide_ens[pl.ds(k, cells // MARGIN, stride=local), :].astype(BF16)
        found = dot_tn(values, in_column)
        gathered.append(jnp.sum(jnp.where(in_lane, found, 0.0), axis=0, keepdims=True))
    at_buf[rows(me), :] = jnp.concatenate(gathered, axis=0).astype(BF16)
    bord[region] = ens_ref[:, pl.ds(0, MARGIN)]

    pl.semaphore_wait(barrier, zs + ys + n - 3)
    up = remote(bl_ref, bl_buf.at[0], bl_send.at[0], bl_recv.at[0], member=lax.rem(me + 1, n))
    down = remote(bl_ref, bl_buf.at[1], bl_send.at[1], bl_recv.at[1], member=lax.rem(me + n - 1, n))
    lax.fori_loop(1, zs, started(z_copy), 0)
    lax.fori_loop(1, n, started(at_copy), 0)
    lax.fori_loop(1, zs, arrived(z_copy), 0)
    lax.fori_loop(1, ys, started(y_copy), 0)

    holder = (target // cells).astype(F32)
    s_low = jnp.min(jnp.where(is_local, 1e6, holder), axis=1, keepdims=True)
    s_high = jnp.max(jnp.where(is_local, -1.0, holder), axis=1, keepdims=True)
    lax.fori_loop(1, ys, arrived(y_copy), 0)

    def pick(s, c):
        low, high = c
        block = bord[s].astype(F32)
        at = s.astype(F32)
        return jnp.where(s_low == at, block, low), jnp.where(s_high == at, block, high)

    nothing = jnp.zeros((local, MARGIN), F32)
    low, high = lax.fori_loop(0, regions, pick, (nothing, nothing), unroll=8)
    mine = jnp.concatenate([low, high], axis=1).astype(BF16)
    fwd[...] = mine
    picked[rows(me), :] = mine
    lax.fori_loop(1, n, started(fw_copy), 0)

    lax.fori_loop(1, n, started(ce_copy), 0)
    up.start()
    down.start()
    cells_buf[rows(me), :] = ens_ref[:, pl.ds(cell_start(me), 4 * half)]

    def extra_copy(k):
        d = (1, n - 2)[k]
        source = ens_ref.at[:, pl.ds((0, cells - half)[k], half)]
        return remote(source, extra_buf.at[rows(me)], xs_send.at[k], xs_recv.at[me], member=d)

    for k, d in enumerate((1, n - 2)):
        @pl.when(me != d)
        def _():
            extra_copy(k).start()

        @pl.when(me == d)
        def _():
            extra_buf[rows(me), :] = ens_ref[:, pl.ds((0, cells - half)[k], half)]

    within = lax.rem(target, cells)
    key = jnp.where(
        is_local, -1,
        jnp.where(holder == s_low, within, jnp.where(holder == s_high, MARGIN + within, -1)),
    )
    onehot = (lax.broadcasted_iota(jnp.int32, (2 * MARGIN, slots), 0) == key).astype(F32).astype(BF16)
    active = lax.broadcasted_iota(jnp.int32, (1, slots), 1) < count_ref[0]
    weights = jnp.where(active, rw_ref[...], 0.0)
    points = weights.shape[0]
    pair = jnp.concatenate([weights, weights * rep_ref[...]], axis=0)
    by_cell = dot_nt(jnp.concatenate(split(pair), axis=0), onehot)
    by_cell = by_cell[:2 * points] + by_cell[2 * points:]
    cell_weights, cell_reports = by_cell[:points], by_cell[points:]
    padding = jnp.zeros((MARGIN - points, slots), F32)

    lax.fori_loop(1, n, arrived(at_copy), 0)
    at_reports = at_buf[...].astype(F32)
    mean = jnp.sum(at_reports, axis=0, keepdims=True) * (1.0 / members)
    pert = (at_reports - mean).astype(BF16)
    pert_wide = pert.astype(F32)
    departure = jnp.concatenate([weights * (rep_ref[...] - mean), padding], axis=0).astype(BF16)
    forcing_s[...] = dot_nt(pert, departure)
    for q in range(points):
        x_s[q] = dot_nt((pert_wide * weights[q:q + 1]).astype(BF16), pert)

    lax.fori_loop(1, n, arrived(fw_copy), 0)
    values = picked[...].astype(F32)
    mean = jnp.sum(values, axis=0, keepdims=True) * (1.0 / members)
    pert = (values - mean).astype(BF16)
    pert_wide = pert.astype(F32)
    departure = jnp.concatenate([cell_reports - cell_weights * mean, padding[:, :2 * MARGIN]], axis=0).astype(BF16)
    forcing = forcing_s[...] + dot_nt(pert, departure)
    eye = (
        lax.broadcasted_iota(jnp.int32, (members, members), 0)
        == lax.broadcasted_iota(jnp.int32, (members, members), 1)
    ).astype(F32)

    def total(v):
        return jnp.sum(jnp.sum(v, axis=0, keepdims=True), axis=1, keepdims=True)

    scales = []
    for q in range(points):
        weighted = (pert_wide * cell_weights[q:q + 1]).astype(BF16)
        precision_mat = (members - 1.0) * eye + x_s[q] + dot_nt(weighted, pert)
        frob = jnp.sqrt(total(precision_mat * precision_mat))
        c = total(precision_mat * eye) * (1.0 / members) / frob
        x_s[q] = precision_mat * (1.0 / frob) - c * eye
        scales.append((frob, c))

    centres = [c for _, c in scales]
    gains = [1.0 for _ in scales]
    for sweep in range(4):
        for q in range(points):
            e_part = x_s[q]
            narrow_e = e_part.astype(BF16)
            c, g = centres[q], gains[q]
            d = 1.5 - 0.5 * c
            if sweep:
                j_part = z_s[q]
                j_next = d * j_part - (0.5 * g) * e_part - 0.5 * dot(j_part.astype(BF16), narrow_e)
            else:
                j_next = -0.5 * e_part
            gains[q] = g * d
            if sweep < 3:
                h_part = (d - 0.5 * c) * e_part - 0.5 * dot(narrow_e, narrow_e)
                x_s[q] = d * h_part - (0.5 * c * d) * e_part - 0.5 * dot(h_part.astype(BF16), narrow_e)
                centres[q] = c * d * d
            z_s[q] = j_next
    for q in range(points):
        root = gains[q] * eye + z_s[q]
        frob = scales[q][0]
        step = jnp.sum(root * forcing[:, q:q + 1], axis=0, keepdims=True)
        mean_weights = jnp.sum(root * step, axis=1, keepdims=True) * (1.0 / frob)
        t_s[q] = (mean_weights + (math.sqrt(members - 1.0) * lax.rsqrt(frob)) * root).astype(BF16)

    lax.fori_loop(1, n, arrived(ce_copy), 0)

    def turn(values):
        across = values.astype(F32).T
        mean = jnp.sum(across, axis=1, keepdims=True) * (1.0 / members)
        return mean, (across - mean).astype(BF16)

    for b in range(4):
        cut = slice(b * half, (b + 1) * half)
        mean_col[cut], anom[cut] = turn(cells_buf[:, cut])

    up.wait_recv()
    down.wait_recv()

    def mixed(values):
        return values * (1.0 / jnp.sum(values, axis=0, keepdims=True))

    own, below, above = mixed(bl_ref[...]), mixed(bl_buf[0]), mixed(bl_buf[1])
    weights_of = [
        below[2:4, half:],
        jnp.where(me == 0, own[0:2, :half], own[2:4, :half]),
        jnp.where(me == n - 1, own[2:4, half:], own[0:2, half:]),
        above[0:2, :half],
        jnp.where(me == 1, below[2:4, :half], above[0:2, half:]),
    ]
    stacked = jnp.concatenate(weights_of + [jnp.zeros((MARGIN - 10, half), F32)], axis=0)
    mix = stacked.T

    narrow, wide = 3 * half // 8, 5 * half // 8

    def blended(values, b):
        w0, w1 = mix[:, 2 * b:2 * b + 1], mix[:, 2 * b + 1:2 * b + 2]
        s0 = dot(values[:narrow], t_s[0])
        s1 = dot(values[:wide], t_s[1])
        s2 = dot(values[narrow:], t_s[2])
        s3 = dot(values[wide:], t_s[3])
        return jnp.concatenate([
            w0[:narrow] * s0 + w1[:narrow] * s1[:narrow],
            w0[narrow:wide] * s1[narrow:] + w1[narrow:wide] * s2[:wide - narrow],
            w0[wide:] * s2[wide - narrow:] + w1[wide:] * s3,
        ], axis=0)

    base = pl.multiple_of(half * (1 - first + last), half)

    def part(offset):
        return pl.ds(pl.multiple_of(base + offset, half), half)

    def out_copy(k, d, side):
        return remote(sent.at[k], got.at[side], cn_send.at[k], cn_recv.at[side], member=d)

    @pl.when(me < n - 1)
    def _():
        sent[0] = blended(anom[part(2 * half)], 3).astype(BF16)
        out_copy(0, me + 1, 0).start()

    @pl.when(me > 0)
    def _():
        sent[1] = blended(anom[part(-half)], 0).astype(BF16)
        out_copy(1, me - 1, 1).start()

    for k, d, target_d, side in ((0, 1, 0, 0), (1, n - 2, n - 1, 1)):
        @pl.when(me == d)
        def _():
            def extra_in(i, c):
                src = peer(i)
                remote(
                    ens_ref.at[:, pl.ds(0, half)], extra_buf.at[rows(src)], xs_send.at[k], xs_recv.at[src], member=src
                ).wait_recv()
                return c

            lax.fori_loop(1, n, extra_in, 0)
            sent[2] = blended(turn(extra_buf[...])[1], 4).astype(BF16)
            out_copy(2, target_d, side).start()

    mine_0 = mean_col[part(0)] + blended(anom[part(0)], 1)
    mine_1 = mean_col[part(half)] + blended(anom[part(half)], 2)
    lax.fori_loop(1, zs, sent_off(z_copy), 0)
    lax.fori_loop(1, ys, sent_off(y_copy), 0)
    lax.fori_loop(1, n, sent_off(at_copy), 0)
    lax.fori_loop(1, n, sent_off(fw_copy), 0)
    lax.fori_loop(1, n, sent_off(ce_copy), 0)
    up.wait_send()
    down.wait_send()
    for k, d in enumerate((1, n - 2)):
        @pl.when(me != d)
        def _():
            extra_copy(k).wait_send()

        @pl.when(me == d)
        def _():
            out_copy(2, 0, 0).wait_send()

    @pl.when(me < n - 1)
    def _():
        out_copy(0, me + 1, 0).wait_send()

    @pl.when(me > 0)
    def _():
        out_copy(1, me - 1, 1).wait_send()

    out_copy(0, lax.rem(me + 1, n), 0).wait_recv()
    out_ref[:half] = (mine_0 + got[0].astype(F32)).astype(BF16)
    out_copy(1, lax.rem(me + n - 1, n), 1).wait_recv()
    out_ref[half:] = (mine_1 + got[1].astype(F32)).astype(BF16)


def per_device(ensemble, reports, report_count, report_cell, report_weight, blending):
    local, cells = ensemble.shape
    n = lax.axis_size("member")
    members = n * local
    slots = reports.shape[1]
    regions, zs = lax.axis_size("region"), Z_CHIPS
    points = report_weight.shape[1]
    half = cells // n // 2
    vmem = pl.BlockSpec(memory_space=pltpu.VMEM)
    anywhere = pl.BlockSpec(memory_space=pltpu.HBM)
    dma = pltpu.SemaphoreType.DMA
    return pl.pallas_call(
        kernel,
        out_shape=jax.ShapeDtypeStruct((cells // n, members), BF16),
        in_specs=[anywhere] * 6,
        out_specs=vmem,
        scratch_shapes=[
            pltpu.SMEM((1,), jnp.int32),
            pltpu.VMEM((local, cells), BF16),
            pltpu.VMEM((1, slots), F32),
            pltpu.VMEM((1, slots), jnp.int32),
            pltpu.VMEM((points, slots), F32),
            pltpu.VMEM((4, 2 * half), F32),
            dma((6,)),
            pltpu.VMEM((members, slots), BF16),
            pltpu.VMEM((members, 4 * half), BF16),
            pltpu.VMEM((members, half), BF16),
            pltpu.VMEM((2, 4, 2 * half), F32),
            pltpu.VMEM((regions, local, MARGIN), BF16),
            pltpu.VMEM((local, 2 * MARGIN), BF16),
            pltpu.VMEM((members, 2 * MARGIN), BF16),
            pltpu.VMEM((3, half, members), BF16),
            pltpu.VMEM((2, half, members), BF16),
            pltpu.VMEM((4 * half, members), BF16),
            pltpu.VMEM((half, members), BF16),
            pltpu.VMEM((4 * half, 1), F32),
            pltpu.VMEM((local * cells // MARGIN, MARGIN), F32),
            pltpu.VMEM((points, members, members), F32),
            pltpu.VMEM((points, members, members), F32),
            pltpu.VMEM((points, members, members), BF16),
            pltpu.VMEM((members, MARGIN), F32),
            dma((zs,)), dma((zs,)), dma((regions // zs,)), dma((regions // zs,)), dma((n,)), dma((n,)), dma((n,)), dma((n,)), dma((n,)), dma((n,)),
            dma((2,)), dma((2,)), dma((2,)), dma((n,)), dma((3,)), dma((2,)),
        ],
        compiler_params=pltpu.CompilerParams(
            collective_id=0, has_side_effects=True, vmem_limit_bytes=48 * 1024 * 1024
        ),
    )(report_count, *(pltpu.with_memory_space_constraint(v, pltpu.HBM) for v in (ensemble, reports, report_cell, report_weight[0], blending)))


def solution(mesh):
    return jax.shard_map(
        per_device,
        mesh=mesh,
        in_specs=(
            P("member", "region"),
            P("region", None),
            P("region"),
            P("region", None),
            P("region", "member", None),
            P(None, ("region", "member")),
        ),
        out_specs=P(("region", "member"), None),
        check_vma=False,
    )
```

```python
import functools
import math

import jax
import jax.numpy as jnp
from jax import lax
from jax.experimental import pallas as pl
from jax.experimental.pallas import tpu as pltpu
from jax.sharding import PartitionSpec as P

MESH = pl.DeviceIdType.MESH
MARGIN = 128
Z_CHIPS = 4
F32 = jnp.float32
BF16 = jnp.bfloat16


def split(value):
    high = value.astype(BF16)
    low = (value - high.astype(F32)).astype(BF16)
    return high, low


def dot(a, b):
    return jnp.dot(a, b, preferred_element_type=F32)


def dot_nt(a, b):
    return lax.dot_general(a, b, (((1,), (1,)), ((), ())), preferred_element_type=F32)


def dot_tn(a, b):
    return lax.dot_general(a, b, (((0,), (0,)), ((), ())), preferred_element_type=F32)


def kernel(
    count_hbm, ens_hbm, rep_hbm, cell_hbm, rw_hbm, bl_hbm, out_ref,
    count_ref, ens_ref, rep_ref, cell_ref, rw_ref, bl_ref, in_sem,
    at_buf, cells_buf, extra_buf, bl_buf, bord, fwd, picked, sent, got, mix_s,
    wide_ens, x_s, z_s, t_s, forcing_s,
    by_send, by_recv, dn_send, dn_recv, pu_send, pu_recv, ready, at_send, at_recv, ce_send, ce_recv, fw_send, fw_recv,
    bl_send, bl_recv, xs_send, xs_recv, cn_send, cn_recv,
):
    region = lax.axis_index("region")
    me = lax.axis_index("member")
    local, cells = ens_ref.shape
    zs = Z_CHIPS
    n = 16
    members = n * local
    regions = bord.shape[0]
    ys = regions // zs
    y, z = region // zs, region % zs
    half = cells // n // 2
    slots = at_buf.shape[1]
    first = (n - 1 - me) // (n - 1)
    last = me // (n - 1)

    def peer(i):
        return lax.rem(me + i, n)

    later = zs - 1 - z

    def at_row(i, plane):
        return lax.rem(y + i, ys) * zs + plane

    def y_peer(i):
        return at_row(i, z)

    def rows(d):
        return pl.ds(pl.multiple_of(d * local, local), local)

    def remote(src, dst, ss, rs, **where):
        return pltpu.make_async_remote_copy(
            src_ref=src, dst_ref=dst, send_sem=ss, recv_sem=rs, device_id=where, device_id_type=MESH
        )

    own_block = z * ys + y
    edge_hbm = ens_hbm.at[:, pl.ds(0, MARGIN)]
    own_plane = bord.at[pl.ds(z * ys, ys)]

    def y_copy(i):
        return remote(edge_hbm, bord.at[own_block], by_send.at[i], by_recv.at[i], region=y_peer(i))

    def down_copy(t):
        where = at_row(lax.rem(t, ys), z - t // ys)
        return remote(edge_hbm, bord.at[own_block], dn_send.at[t], dn_recv.at[t], region=where)

    def start_down(t, c):
        down_copy(ys * (z - t // ys) + lax.rem(t, ys)).start()
        return c

    def down_arrival(t):
        return remote(edge_hbm, bord.at[own_block], dn_send.at[t], dn_recv.at[t], region=y_peer(1))

    def up_copy(k):
        return remote(own_plane, own_plane, pu_send.at[k], pu_recv.at[k], region=y * zs + z + k)

    def up_arrival(k):
        return remote(own_plane, own_plane, pu_send.at[k], pu_recv.at[k], region=y_peer(1))

    def at_copy(i):
        block = at_buf.at[rows(me)]
        return remote(block, block, at_send.at[i], at_recv.at[i], member=peer(i))

    def cell_start(d):
        return pl.multiple_of(2 * half * d - half + half * ((n - 1 - d) // (n - 1)) - half * (d // (n - 1)), MARGIN)

    def ce_copy(i):
        source = ens_ref.at[:, pl.ds(cell_start(peer(i)), 4 * half)]
        return remote(source, cells_buf.at[rows(me)], ce_send.at[i], ce_recv.at[i], member=peer(i))

    def fw_copy(i):
        return remote(fwd, picked.at[rows(me)], fw_send.at[i], fw_recv.at[i], member=peer(i))

    def started(copy):
        def body(i, c):
            copy(i).start()
            return c
        return body

    def sent_off(copy):
        def body(i, c):
            copy(i).wait_send()
            return c
        return body

    def arrived(copy):
        def body(i, c):
            copy(i).wait_recv()
            return c
        return body

    barrier = pltpu.get_barrier_semaphore()

    def greet(i, c):
        pl.semaphore_signal(barrier, inc=1, device_id={"member": peer(i)}, device_id_type=MESH)
        return c

    def greet_later(t, c):
        where = at_row(lax.rem(t, ys), z + t // ys)
        pl.semaphore_signal(barrier, inc=1, device_id={"region": where}, device_id_type=MESH)
        return c

    def say_ready(k, c):
        pl.semaphore_signal(ready.at[k], inc=1, device_id={"region": y * zs + z - k}, device_id_type=MESH)
        return c

    def greet_y(i, c):
        pl.semaphore_signal(barrier, inc=1, device_id={"region": y_peer(i)}, device_id_type=MESH)
        return c

    lax.fori_loop(1, ys, greet_y, 0)
    lax.fori_loop(1, n, greet, 0)
    loads = [
        pltpu.make_async_copy(source, landed, in_sem.at[i])
        for i, (source, landed) in enumerate((
            (ens_hbm, ens_ref), (cell_hbm, cell_ref), (bl_hbm, bl_ref), (rw_hbm, rw_ref), (rep_hbm, rep_ref), (count_hbm, count_ref)
        ))
    ]
    for load in loads:
        load.start()
    lax.fori_loop(ys, ys + ys * later, greet_later, 0)
    pl.semaphore_wait(barrier, ys + n - 2 + ys * z)
    lax.fori_loop(1, 1 + z, say_ready, 0)
    lax.fori_loop(0, ys * z, start_down, 0)
    lax.fori_loop(1, ys, started(y_copy), 0)
    for load in loads:
        load.wait()
    bord[own_block] = ens_ref[:, pl.ds(0, MARGIN)]

    target = cell_ref[...]
    relative = target - region * cells
    is_local = (relative >= 0) & (relative < cells)
    lane = lax.rem(jnp.where(is_local, relative, 0), MARGIN)
    column = jnp.where(is_local, relative // MARGIN, -1)
    for h in range(cells // MARGIN):
        wide_ens[h * local:(h + 1) * local, :] = ens_ref[:, h * MARGIN:(h + 1) * MARGIN].astype(F32)
    in_column = (lax.broadcasted_iota(jnp.int32, (cells // MARGIN, slots), 0) == column).astype(F32).astype(BF16)
    in_lane = lax.broadcasted_iota(jnp.int32, (MARGIN, slots), 0) == lane
    gathered = []
    for k in range(local):
        values = wide_ens[pl.ds(k, cells // MARGIN, stride=local), :].astype(BF16)
        found = dot_tn(values, in_column)
        gathered.append(jnp.sum(jnp.where(in_lane, found, 0.0), axis=0, keepdims=True))
    at_buf[rows(me), :] = jnp.concatenate(gathered, axis=0).astype(BF16)

    up = remote(bl_ref, bl_buf.at[0], bl_send.at[0], bl_recv.at[0], member=lax.rem(me + 1, n))
    down = remote(bl_ref, bl_buf.at[1], bl_send.at[1], bl_recv.at[1], member=lax.rem(me + n - 1, n))
    up.start()
    down.start()
    lax.fori_loop(1, n, started(at_copy), 0)
    lax.fori_loop(1, n, started(ce_copy), 0)

    holder = (target // cells).astype(F32)
    s_low = jnp.min(jnp.where(is_local, 1e6, holder), axis=1, keepdims=True)
    s_high = jnp.max(jnp.where(is_local, -1.0, holder), axis=1, keepdims=True)

    def pick(plane, row, found):
        low, high = found
        block = bord[plane * ys + row].astype(F32)
        at = (row * zs + plane).astype(F32)
        return jnp.where(s_low == at, block, low), jnp.where(s_high == at, block, high)

    def pick_row(i, found):
        y_copy(i).wait_recv()
        return pick(z, lax.rem(y + ys - i, ys), found)

    def send_up(k, c):
        pl.semaphore_wait(ready.at[k], 1)
        up_copy(k).start()
        return c

    def pick_later(t, found):
        down_arrival(t).wait_recv()
        return pick(z + t // ys, lax.rem(y + ys - lax.rem(t, ys), ys), found)

    def pick_earlier(k, found):
        up_arrival(k).wait_recv()
        for row in range(ys):
            found = pick(z - k, row, found)
        return found

    nothing = jnp.zeros((local, MARGIN), F32)
    found = pick(z, y, (nothing, nothing))
    found = lax.fori_loop(1, ys, pick_row, found)
    lax.fori_loop(1, 1 + later, send_up, 0)
    found = lax.fori_loop(ys, ys + ys * later, pick_later, found)
    low, high = lax.fori_loop(1, 1 + z, pick_earlier, found)
    mine = jnp.concatenate([low, high], axis=1).astype(BF16)
    fwd[...] = mine
    picked[rows(me), :] = mine
    lax.fori_loop(1, n, started(fw_copy), 0)

    cells_buf[rows(me), :] = ens_ref[:, pl.ds(cell_start(me), 4 * half)]

    def extra_copy(k):
        d = (1, n - 2)[k]
        source = ens_ref.at[:, pl.ds((0, cells - half)[k], half)]
        return remote(source, extra_buf.at[rows(me)], xs_send.at[k], xs_recv.at[me], member=d)

    for k, d in enumerate((1, n - 2)):
        @pl.when(me != d)
        def _():
            extra_copy(k).start()

        @pl.when(me == d)
        def _():
            extra_buf[rows(me), :] = ens_ref[:, pl.ds((0, cells - half)[k], half)]

    within = lax.rem(target, cells)
    key = jnp.where(
        is_local, -1,
        jnp.where(holder == s_low, within, jnp.where(holder == s_high, MARGIN + within, -1)),
    )
    onehot = (lax.broadcasted_iota(jnp.int32, (2 * MARGIN, slots), 0) == key).astype(F32).astype(BF16)
    active = lax.broadcasted_iota(jnp.int32, (1, slots), 1) < count_ref[0]
    weights = jnp.where(active, rw_ref[...], 0.0)
    points = weights.shape[0]
    pair = jnp.concatenate([weights, weights * rep_ref[...]], axis=0)
    by_cell = dot_nt(jnp.concatenate(split(pair), axis=0), onehot)
    by_cell = by_cell[:2 * points] + by_cell[2 * points:]
    cell_weights, cell_reports = by_cell[:points], by_cell[points:]
    padding = jnp.zeros((MARGIN - points, slots), F32)

    lax.fori_loop(1, n, arrived(at_copy), 0)
    at_reports = at_buf[...].astype(F32)
    mean = jnp.sum(at_reports, axis=0, keepdims=True) * (1.0 / members)
    pert = (at_reports - mean).astype(BF16)
    pert_wide = pert.astype(F32)
    departure = jnp.concatenate([weights * (rep_ref[...] - mean), padding], axis=0).astype(BF16)
    forcing_s[...] = dot_nt(pert, departure)
    for q in range(points):
        x_s[q] = dot_nt((pert_wide * weights[q:q + 1]).astype(BF16), pert)

    up.wait_recv()
    down.wait_recv()

    def mixed(values):
        return values * (1.0 / jnp.sum(values, axis=0, keepdims=True))

    own, below, above = mixed(bl_ref[...]), mixed(bl_buf[0]), mixed(bl_buf[1])
    weights_of = [
        below[2:4, half:],
        jnp.where(me == 0, own[0:2, :half], own[2:4, :half]),
        jnp.where(me == n - 1, own[2:4, half:], own[0:2, half:]),
        above[0:2, :half],
        jnp.where(me == 1, below[2:4, :half], above[0:2, half:]),
    ]
    stacked = jnp.concatenate(weights_of + [jnp.zeros((MARGIN - 10, half), F32)], axis=0)
    mix_s[...] = stacked.T

    lax.fori_loop(1, n, arrived(fw_copy), 0)
    values = picked[...].astype(F32)
    mean = jnp.sum(values, axis=0, keepdims=True) * (1.0 / members)
    pert = (values - mean).astype(BF16)
    pert_wide = pert.astype(F32)
    departure = jnp.concatenate([cell_reports - cell_weights * mean, padding[:, :2 * MARGIN]], axis=0).astype(BF16)
    forcing = forcing_s[...] + dot_nt(pert, departure)
    eye = (
        lax.broadcasted_iota(jnp.int32, (members, members), 0)
        == lax.broadcasted_iota(jnp.int32, (members, members), 1)
    ).astype(F32)

    def total(v):
        return jnp.sum(jnp.sum(v, axis=0, keepdims=True), axis=1, keepdims=True)

    block_eye = eye[:MARGIN, :MARGIN]
    frobs, centres = [], []
    for q in range(points):
        weighted = (pert_wide * cell_weights[q:q + 1]).astype(BF16)
        precision_mat = (members - 1.0) * eye + x_s[q] + dot_nt(weighted, pert)
        trace = sum(
            total(precision_mat[k:k + MARGIN, k:k + MARGIN] * block_eye) for k in range(0, members, MARGIN)
        ) * (1.0 / members)
        frob = jnp.sqrt(total(precision_mat * precision_mat))
        x_s[q] = precision_mat * (1.0 / trace) - eye
        frobs.append(frob)
        centres.append(trace / frob)

    gains = [1.0 for _ in frobs]
    for sweep in range(4):
        for q in range(points):
            f_part = x_s[q]
            d = 1.5 - 0.5 * centres[q]
            away = (0.5 * centres[q] / d) * f_part
            narrow = away.astype(BF16)
            if sweep:
                k_part = z_s[q]
                z_s[q] = k_part - away - dot(k_part.astype(BF16), narrow)
            else:
                z_s[q] = -away
            if sweep < 3:
                h_part = f_part - away - dot(f_part.astype(BF16), narrow)
                x_s[q] = h_part - away - dot(h_part.astype(BF16), narrow)
            gains[q] = gains[q] * d
            centres[q] = centres[q] * d * d
    for q in range(points):
        root = eye + z_s[q]
        frob, gain = frobs[q], gains[q]
        step = jnp.sum(root * forcing[:, q:q + 1], axis=0, keepdims=True)
        mean_weights = jnp.sum(root * step, axis=1, keepdims=True) * (gain * gain / frob)
        t_s[q] = (mean_weights + (math.sqrt(members - 1.0) * gain * lax.rsqrt(frob)) * root).astype(BF16)

    lax.fori_loop(1, n, arrived(ce_copy), 0)

    def turn(values):
        across = values.astype(F32).T
        mean = jnp.sum(across, axis=1, keepdims=True) * (1.0 / members)
        return mean, (across - mean).astype(BF16)

    mix = mix_s[...]

    narrow, wide = 3 * half // 8, 5 * half // 8

    def blended(values, b):
        w0, w1 = mix[:, 2 * b:2 * b + 1], mix[:, 2 * b + 1:2 * b + 2]
        s0 = dot(values[:narrow], t_s[0])
        s1 = dot(values[:wide], t_s[1])
        s2 = dot(values[narrow:], t_s[2])
        s3 = dot(values[wide:], t_s[3])
        return jnp.concatenate([
            w0[:narrow] * s0 + w1[:narrow] * s1[:narrow],
            w0[narrow:wide] * s1[narrow:] + w1[narrow:wide] * s2[:wide - narrow],
            w0[wide:] * s2[wide - narrow:] + w1[wide:] * s3,
        ], axis=0)

    base = pl.multiple_of(half * (1 - first + last), half)

    def part(offset):
        return pl.ds(pl.multiple_of(base + offset, half), half)

    def out_copy(k, d, side):
        return remote(sent.at[k], got.at[side], cn_send.at[k], cn_recv.at[side], member=d)

    @pl.when(me < n - 1)
    def _():
        sent[0] = blended(turn(cells_buf[:, part(2 * half)])[1], 3).astype(BF16)
        out_copy(0, me + 1, 0).start()

    @pl.when(me > 0)
    def _():
        sent[1] = blended(turn(cells_buf[:, part(-half)])[1], 0).astype(BF16)
        out_copy(1, me - 1, 1).start()

    for k, d, target_d, side in ((0, 1, 0, 0), (1, n - 2, n - 1, 1)):
        @pl.when(me == d)
        def _():
            def extra_in(i, c):
                src = peer(i)
                remote(
                    ens_ref.at[:, pl.ds(0, half)], extra_buf.at[rows(src)], xs_send.at[k], xs_recv.at[src], member=src
                ).wait_recv()
                return c

            lax.fori_loop(1, n, extra_in, 0)
            sent[2] = blended(turn(extra_buf[...])[1], 4).astype(BF16)
            out_copy(2, target_d, side).start()

    cell_mean, anomaly = turn(cells_buf[:, part(0)])
    mine_0 = cell_mean + blended(anomaly, 1)
    cell_mean, anomaly = turn(cells_buf[:, part(half)])
    mine_1 = cell_mean + blended(anomaly, 2)

    lax.fori_loop(1, ys, sent_off(y_copy), 0)
    lax.fori_loop(ys, ys + ys * z, sent_off(down_copy), 0)
    lax.fori_loop(1, 1 + later, sent_off(up_copy), 0)
    lax.fori_loop(1, n, sent_off(at_copy), 0)
    lax.fori_loop(1, n, sent_off(fw_copy), 0)
    lax.fori_loop(1, n, sent_off(ce_copy), 0)
    up.wait_send()
    down.wait_send()
    for k, d in enumerate((1, n - 2)):
        @pl.when(me != d)
        def _():
            extra_copy(k).wait_send()

        @pl.when(me == d)
        def _():
            out_copy(2, 0, 0).wait_send()

    @pl.when(me < n - 1)
    def _():
        out_copy(0, me + 1, 0).wait_send()

    @pl.when(me > 0)
    def _():
        out_copy(1, me - 1, 1).wait_send()

    out_copy(0, lax.rem(me + 1, n), 0).wait_recv()
    out_ref[:half] = (mine_0 + got[0].astype(F32)).astype(BF16)
    out_copy(1, lax.rem(me + n - 1, n), 1).wait_recv()
    out_ref[half:] = (mine_1 + got[1].astype(F32)).astype(BF16)


def per_device(ensemble, reports, report_count, report_cell, report_weight, blending):
    local, cells = ensemble.shape
    n = lax.axis_size("member")
    members = n * local
    slots = reports.shape[1]
    regions, zs = lax.axis_size("region"), Z_CHIPS
    points = report_weight.shape[1]
    half = cells // n // 2
    vmem = pl.BlockSpec(memory_space=pltpu.VMEM)
    anywhere = pl.BlockSpec(memory_space=pltpu.HBM)
    dma = pltpu.SemaphoreType.DMA
    return pl.pallas_call(
        kernel,
        out_shape=jax.ShapeDtypeStruct((cells // n, members), BF16),
        in_specs=[anywhere] * 6,
        out_specs=vmem,
        scratch_shapes=[
            pltpu.SMEM((1,), jnp.int32),
            pltpu.VMEM((local, cells), BF16),
            pltpu.VMEM((1, slots), F32),
            pltpu.VMEM((1, slots), jnp.int32),
            pltpu.VMEM((points, slots), F32),
            pltpu.VMEM((4, 2 * half), F32),
            dma((6,)),
            pltpu.VMEM((members, slots), BF16),
            pltpu.VMEM((members, 4 * half), BF16),
            pltpu.VMEM((members, half), BF16),
            pltpu.VMEM((2, 4, 2 * half), F32),
            pltpu.VMEM((regions, local, MARGIN), BF16),
            pltpu.VMEM((local, 2 * MARGIN), BF16),
            pltpu.VMEM((members, 2 * MARGIN), BF16),
            pltpu.VMEM((3, half, members), BF16),
            pltpu.VMEM((2, half, members), BF16),
            pltpu.VMEM((half, MARGIN), F32),
            pltpu.VMEM((local * cells // MARGIN, MARGIN), F32),
            pltpu.VMEM((points, members, members), F32),
            pltpu.VMEM((points, members, members), F32),
            pltpu.VMEM((points, members, members), BF16),
            pltpu.VMEM((members, MARGIN), F32),
            dma((regions // zs,)), dma((regions // zs,)), dma((regions,)), dma((regions,)), dma((zs,)), dma((zs,)),
            pltpu.SemaphoreType.REGULAR((zs,)), dma((n,)), dma((n,)), dma((n,)), dma((n,)), dma((n,)), dma((n,)),
            dma((2,)), dma((2,)), dma((2,)), dma((n,)), dma((3,)), dma((2,)),
        ],
        compiler_params=pltpu.CompilerParams(
            collective_id=0, has_side_effects=True, vmem_limit_bytes=48 * 1024 * 1024
        ),
    )(report_count, *(pltpu.with_memory_space_constraint(v, pltpu.HBM) for v in (ensemble, reports, report_cell, report_weight[0], blending)))


def solution(mesh):
    return jax.shard_map(
        per_device,
        mesh=mesh,
        in_specs=(
            P("member", "region"),
            P("region", None),
            P("region"),
            P("region", None),
            P("region", "member", None),
            P(None, ("region", "member")),
        ),
        out_specs=P(("region", "member"), None),
        check_vma=False,
    )
```

```python
import functools
import math

import jax
import jax.numpy as jnp
from jax import lax
from jax.experimental import pallas as pl
from jax.experimental.pallas import tpu as pltpu
from jax.sharding import PartitionSpec as P

MESH = pl.DeviceIdType.MESH
MARGIN = 128
Z_CHIPS = 4
F32 = jnp.float32
BF16 = jnp.bfloat16


def split(value):
    high = value.astype(BF16)
    low = (value - high.astype(F32)).astype(BF16)
    return high, low


def dot(a, b):
    return jnp.dot(a, b, preferred_element_type=F32)


def dot_nt(a, b):
    return lax.dot_general(a, b, (((1,), (1,)), ((), ())), preferred_element_type=F32)


def dot_tn(a, b):
    return lax.dot_general(a, b, (((0,), (0,)), ((), ())), preferred_element_type=F32)


def kernel(
    count_hbm, ens_hbm, rep_hbm, cell_hbm, rw_hbm, bl_hbm, out_ref,
    count_ref, ens_ref, rep_ref, cell_ref, rw_ref, bl_ref, in_sem,
    at_buf, cells_buf, extra_buf, bl_buf, bord, fwd, picked, sent, got, mix_s,
    wide_ens, x_s, z_s, t_s, forcing_s,
    by_send, by_recv, dn_send, dn_recv, pu_send, pu_recv, ready, at_send, at_recv, ce_send, ce_recv, fw_send, fw_recv,
    bl_send, bl_recv, xs_send, xs_recv, cn_send, cn_recv,
):
    region = lax.axis_index("region")
    me = lax.axis_index("member")
    local, cells = ens_ref.shape
    zs = Z_CHIPS
    n = 16
    members = n * local
    regions = bord.shape[0]
    ys = regions // zs
    y, z = region // zs, region % zs
    half = cells // n // 2
    slots = at_buf.shape[1]
    first = (n - 1 - me) // (n - 1)
    last = me // (n - 1)

    def peer(i):
        return lax.rem(me + i, n)

    later = zs - 1 - z
    lowest = later // (zs - 1)

    def at_row(i, plane):
        return lax.rem(y + i, ys) * zs + plane

    def y_peer(i):
        return at_row(i, z)

    def rows(d):
        return pl.ds(pl.multiple_of(d * local, local), local)

    def remote(src, dst, ss, rs, **where):
        return pltpu.make_async_remote_copy(
            src_ref=src, dst_ref=dst, send_sem=ss, recv_sem=rs, device_id=where, device_id_type=MESH
        )

    own_block = z * ys + y
    edge_hbm = ens_hbm.at[:, pl.ds(0, MARGIN)]
    own_plane = bord.at[pl.ds(z * ys, ys)]

    def y_copy(i):
        return remote(edge_hbm, bord.at[own_block], by_send.at[i], by_recv.at[i], region=y_peer(i))

    def down_copy(t):
        where = at_row(lax.rem(t, ys), z - t // ys)
        return remote(edge_hbm, bord.at[own_block], dn_send.at[t], dn_recv.at[t], region=where)

    def start_down(t, c):
        down_copy(ys * (z - t // ys) + lax.rem(t, ys)).start()
        return c

    def down_arrival(t):
        return remote(edge_hbm, bord.at[own_block], dn_send.at[t], dn_recv.at[t], region=y_peer(1))

    def up_copy(k):
        return remote(own_plane, own_plane, pu_send.at[k], pu_recv.at[k], region=y * zs + z + k)

    def up_arrival(k):
        return remote(own_plane, own_plane, pu_send.at[k], pu_recv.at[k], region=y_peer(1))

    def at_copy(i):
        block = at_buf.at[rows(me)]
        return remote(block, block, at_send.at[i], at_recv.at[i], member=peer(i))

    def cell_start(d):
        return pl.multiple_of(2 * half * d - half + half * ((n - 1 - d) // (n - 1)) - half * (d // (n - 1)), MARGIN)

    def ce_copy(i):
        source = ens_ref.at[:, pl.ds(cell_start(peer(i)), 4 * half)]
        return remote(source, cells_buf.at[rows(me)], ce_send.at[i], ce_recv.at[i], member=peer(i))

    def fw_copy(i):
        return remote(fwd, picked.at[rows(me)], fw_send.at[i], fw_recv.at[i], member=peer(i))

    def started(copy):
        def body(i, c):
            copy(i).start()
            return c
        return body

    def sent_off(copy):
        def body(i, c):
            copy(i).wait_send()
            return c
        return body

    def arrived(copy):
        def body(i, c):
            copy(i).wait_recv()
            return c
        return body

    barrier = pltpu.get_barrier_semaphore()

    def greet(i, c):
        pl.semaphore_signal(barrier, inc=1, device_id={"member": peer(i)}, device_id_type=MESH)
        return c

    def greet_later(t, c):
        where = at_row(lax.rem(t, ys), z + t // ys)
        pl.semaphore_signal(barrier, inc=1, device_id={"region": where}, device_id_type=MESH)
        return c

    def say_ready(k, c):
        pl.semaphore_signal(ready.at[k], inc=1, device_id={"region": y * zs + z - k}, device_id_type=MESH)
        return c

    def greet_y(i, c):
        pl.semaphore_signal(barrier, inc=1, device_id={"region": y_peer(i)}, device_id_type=MESH)
        return c

    lax.fori_loop(1, ys, greet_y, 0)
    lax.fori_loop(1, n, greet, 0)
    loads = [
        pltpu.make_async_copy(source, landed, in_sem.at[i])
        for i, (source, landed) in enumerate((
            (ens_hbm, ens_ref), (cell_hbm, cell_ref), (bl_hbm, bl_ref), (rw_hbm, rw_ref), (rep_hbm, rep_ref), (count_hbm, count_ref)
        ))
    ]
    for load in loads:
        load.start()
    lax.fori_loop(ys, ys + ys * later, greet_later, 0)
    pl.semaphore_wait(barrier, ys + n - 2 + ys * z)
    lax.fori_loop(1, 1 + z, say_ready, 0)
    lax.fori_loop(0, ys * z, start_down, 0)
    lax.fori_loop(1, ys, started(y_copy), 0)
    for load in loads:
        load.wait()
    bord[own_block] = ens_ref[:, pl.ds(0, MARGIN)]

    target = cell_ref[...]
    relative = target - region * cells
    is_local = (relative >= 0) & (relative < cells)
    lane = lax.rem(jnp.where(is_local, relative, 0), MARGIN)
    column = jnp.where(is_local, relative // MARGIN, -1)
    for h in range(cells // MARGIN):
        wide_ens[h * local:(h + 1) * local, :] = ens_ref[:, h * MARGIN:(h + 1) * MARGIN].astype(F32)
    in_column = (lax.broadcasted_iota(jnp.int32, (cells // MARGIN, slots), 0) == column).astype(F32).astype(BF16)
    in_lane = lax.broadcasted_iota(jnp.int32, (MARGIN, slots), 0) == lane
    gathered = []
    for k in range(local):
        values = wide_ens[pl.ds(k, cells // MARGIN, stride=local), :].astype(BF16)
        found = dot_tn(values, in_column)
        gathered.append(jnp.sum(jnp.where(in_lane, found, 0.0), axis=0, keepdims=True))
    at_buf[rows(me), :] = jnp.concatenate(gathered, axis=0).astype(BF16)

    up = remote(bl_ref, bl_buf.at[0], bl_send.at[0], bl_recv.at[0], member=lax.rem(me + 1, n))
    down = remote(bl_ref, bl_buf.at[1], bl_send.at[1], bl_recv.at[1], member=lax.rem(me + n - 1, n))
    up.start()
    down.start()
    lax.fori_loop(1, n, started(at_copy), 0)
    lax.fori_loop(1, 1 + (n - 1) * lowest, started(ce_copy), 0)

    holder = (target // cells).astype(F32)
    s_low = jnp.min(jnp.where(is_local, 1e6, holder), axis=1, keepdims=True)
    s_high = jnp.max(jnp.where(is_local, -1.0, holder), axis=1, keepdims=True)
    wide_low = jnp.broadcast_to(s_low.astype(jnp.int32), (local, MARGIN))
    wide_high = jnp.broadcast_to(s_high.astype(jnp.int32), (local, MARGIN))

    def pick(plane, row, found):
        low, high = found
        block = bord[plane * ys + row].astype(F32)
        at = row * zs + plane
        return jnp.where(wide_low == at, block, low), jnp.where(wide_high == at, block, high)

    def pick_row(i, found):
        y_copy(i).wait_recv()
        return pick(z, lax.rem(y + ys - i, ys), found)

    def send_up(k, c):
        pl.semaphore_wait(ready.at[k], 1)
        up_copy(k).start()
        return c

    def pick_later(t, found):
        down_arrival(t).wait_recv()
        return pick(z + t // ys, lax.rem(y + ys - lax.rem(t, ys), ys), found)

    def pick_earlier(k, found):
        up_arrival(k).wait_recv()
        for row in range(ys):
            found = pick(z - k, row, found)
        return found

    nothing = jnp.zeros((local, MARGIN), F32)
    found = pick(z, y, (nothing, nothing))
    found = lax.fori_loop(1, ys, pick_row, found)
    lax.fori_loop(1, 1 + later, send_up, 0)
    found = lax.fori_loop(ys, ys + ys * later, pick_later, found)
    low, high = lax.fori_loop(1, 1 + z, pick_earlier, found)
    mine = jnp.concatenate([low, high], axis=1).astype(BF16)
    fwd[...] = mine
    picked[rows(me), :] = mine
    lax.fori_loop(1, n, started(fw_copy), 0)
    lax.fori_loop(1, n - (n - 1) * lowest, started(ce_copy), 0)

    cells_buf[rows(me), :] = ens_ref[:, pl.ds(cell_start(me), 4 * half)]

    def extra_copy(k):
        d = (1, n - 2)[k]
        source = ens_ref.at[:, pl.ds((0, cells - half)[k], half)]
        return remote(source, extra_buf.at[rows(me)], xs_send.at[k], xs_recv.at[me], member=d)

    for k, d in enumerate((1, n - 2)):
        @pl.when(me != d)
        def _():
            extra_copy(k).start()

        @pl.when(me == d)
        def _():
            extra_buf[rows(me), :] = ens_ref[:, pl.ds((0, cells - half)[k], half)]

    within = lax.rem(target, cells)
    key = jnp.where(
        is_local, -1,
        jnp.where(holder == s_low, within, jnp.where(holder == s_high, MARGIN + within, -1)),
    )
    onehot = (lax.broadcasted_iota(jnp.int32, (2 * MARGIN, slots), 0) == key).astype(F32).astype(BF16)
    active = lax.broadcasted_iota(jnp.int32, (1, slots), 1) < count_ref[0]
    weights = jnp.where(active, rw_ref[...], 0.0)
    points = weights.shape[0]
    pair = jnp.concatenate([weights, weights * rep_ref[...]], axis=0)
    by_cell = dot_nt(jnp.concatenate(split(pair), axis=0), onehot)
    by_cell = by_cell[:2 * points] + by_cell[2 * points:]
    cell_weights, cell_reports = by_cell[:points], by_cell[points:]
    padding = jnp.zeros((MARGIN - points, slots), F32)

    lax.fori_loop(1, n, arrived(at_copy), 0)
    at_reports = at_buf[...].astype(F32)
    mean = jnp.sum(at_reports, axis=0, keepdims=True) * (1.0 / members)
    pert = (at_reports - mean).astype(BF16)
    pert_wide = pert.astype(F32)
    departure = jnp.concatenate([weights * (rep_ref[...] - mean), padding], axis=0).astype(BF16)
    forcing_s[...] = dot_nt(pert, departure)
    for q in range(points):
        x_s[q] = dot_nt((pert_wide * weights[q:q + 1]).astype(BF16), pert)

    up.wait_recv()
    down.wait_recv()

    def mixed(values):
        return values * (1.0 / jnp.sum(values, axis=0, keepdims=True))

    own, below, above = mixed(bl_ref[...]), mixed(bl_buf[0]), mixed(bl_buf[1])
    weights_of = [
        below[2:4, half:],
        jnp.where(me == 0, own[0:2, :half], own[2:4, :half]),
        jnp.where(me == n - 1, own[2:4, half:], own[0:2, half:]),
        above[0:2, :half],
        jnp.where(me == 1, below[2:4, :half], above[0:2, half:]),
    ]
    stacked = jnp.concatenate(weights_of + [jnp.zeros((MARGIN - 10, half), F32)], axis=0)
    mix_s[...] = stacked.T

    lax.fori_loop(1, n, arrived(fw_copy), 0)
    values = picked[...].astype(F32)
    mean = jnp.sum(values, axis=0, keepdims=True) * (1.0 / members)
    pert = (values - mean).astype(BF16)
    pert_wide = pert.astype(F32)
    departure = jnp.concatenate([cell_reports - cell_weights * mean, padding[:, :2 * MARGIN]], axis=0).astype(BF16)
    forcing = forcing_s[...] + dot_nt(pert, departure)
    eye = (
        lax.broadcasted_iota(jnp.int32, (members, members), 0)
        == lax.broadcasted_iota(jnp.int32, (members, members), 1)
    ).astype(F32)

    def total(v):
        return jnp.sum(jnp.sum(v, axis=0, keepdims=True), axis=1, keepdims=True)

    block_eye = eye[:MARGIN, :MARGIN]
    frobs, centres = [], []
    for q in range(points):
        weighted = (pert_wide * cell_weights[q:q + 1]).astype(BF16)
        precision_mat = (members - 1.0) * eye + x_s[q] + dot_nt(weighted, pert)
        trace = sum(
            total(precision_mat[k:k + MARGIN, k:k + MARGIN] * block_eye) for k in range(0, members, MARGIN)
        ) * (1.0 / members)
        frob = jnp.sqrt(total(precision_mat * precision_mat))
        x_s[q] = precision_mat * (1.0 / trace) - eye
        frobs.append(frob)
        centres.append(trace / frob)

    gains = [1.0 for _ in frobs]
    for sweep in range(4):
        for q in range(points):
            f_part = x_s[q]
            d = 1.5 - 0.5 * centres[q]
            away = (0.5 * centres[q] / d) * f_part
            narrow = away.astype(BF16)
            if sweep:
                k_part = z_s[q]
                z_s[q] = k_part - away - dot(k_part.astype(BF16), narrow)
            else:
                z_s[q] = -away
            if sweep < 3:
                h_part = f_part - away - dot(f_part.astype(BF16), narrow)
                x_s[q] = h_part - away - dot(h_part.astype(BF16), narrow)
            gains[q] = gains[q] * d
            centres[q] = centres[q] * d * d
    for q in range(points):
        root = eye + z_s[q]
        frob, gain = frobs[q], gains[q]
        step = jnp.sum(root * forcing[:, q:q + 1], axis=0, keepdims=True)
        mean_weights = jnp.sum(root * step, axis=1, keepdims=True) * (gain * gain / frob)
        t_s[q] = (mean_weights + (math.sqrt(members - 1.0) * gain * lax.rsqrt(frob)) * root).astype(BF16)

    lax.fori_loop(1, n, arrived(ce_copy), 0)

    def turn(values):
        across = values.astype(F32).T
        mean = jnp.sum(across, axis=1, keepdims=True) * (1.0 / members)
        return mean, (across - mean).astype(BF16)

    mix = mix_s[...]

    narrow, wide = 3 * half // 8, 5 * half // 8

    def blended(values, b):
        w0, w1 = mix[:, 2 * b:2 * b + 1], mix[:, 2 * b + 1:2 * b + 2]
        s0 = dot(values[:narrow], t_s[0])
        s1 = dot(values[:wide], t_s[1])
        s2 = dot(values[narrow:], t_s[2])
        s3 = dot(values[wide:], t_s[3])
        return jnp.concatenate([
            w0[:narrow] * s0 + w1[:narrow] * s1[:narrow],
            w0[narrow:wide] * s1[narrow:] + w1[narrow:wide] * s2[:wide - narrow],
            w0[wide:] * s2[wide - narrow:] + w1[wide:] * s3,
        ], axis=0)

    base = pl.multiple_of(half * (1 - first + last), half)

    def part(offset):
        return pl.ds(pl.multiple_of(base + offset, half), half)

    def out_copy(k, d, side):
        return remote(sent.at[k], got.at[side], cn_send.at[k], cn_recv.at[side], member=d)

    @pl.when(me < n - 1)
    def _():
        sent[0] = blended(turn(cells_buf[:, part(2 * half)])[1], 3).astype(BF16)
        out_copy(0, me + 1, 0).start()

    @pl.when(me > 0)
    def _():
        sent[1] = blended(turn(cells_buf[:, part(-half)])[1], 0).astype(BF16)
        out_copy(1, me - 1, 1).start()

    for k, d, target_d, side in ((0, 1, 0, 0), (1, n - 2, n - 1, 1)):
        @pl.when(me == d)
        def _():
            def extra_in(i, c):
                src = peer(i)
                remote(
                    ens_ref.at[:, pl.ds(0, half)], extra_buf.at[rows(src)], xs_send.at[k], xs_recv.at[src], member=src
                ).wait_recv()
                return c

            lax.fori_loop(1, n, extra_in, 0)
            sent[2] = blended(turn(extra_buf[...])[1], 4).astype(BF16)
            out_copy(2, target_d, side).start()

    cell_mean, anomaly = turn(cells_buf[:, part(0)])
    mine_0 = cell_mean + blended(anomaly, 1)
    cell_mean, anomaly = turn(cells_buf[:, part(half)])
    mine_1 = cell_mean + blended(anomaly, 2)

    lax.fori_loop(1, ys, sent_off(y_copy), 0)
    lax.fori_loop(ys, ys + ys * z, sent_off(down_copy), 0)
    lax.fori_loop(1, 1 + later, sent_off(up_copy), 0)
    lax.fori_loop(1, n, sent_off(at_copy), 0)
    lax.fori_loop(1, n, sent_off(fw_copy), 0)
    lax.fori_loop(1, n, sent_off(ce_copy), 0)
    up.wait_send()
    down.wait_send()
    for k, d in enumerate((1, n - 2)):
        @pl.when(me != d)
        def _():
            extra_copy(k).wait_send()

        @pl.when(me == d)
        def _():
            out_copy(2, 0, 0).wait_send()

    @pl.when(me < n - 1)
    def _():
        out_copy(0, me + 1, 0).wait_send()

    @pl.when(me > 0)
    def _():
        out_copy(1, me - 1, 1).wait_send()

    out_copy(0, lax.rem(me + 1, n), 0).wait_recv()
    out_ref[:half] = (mine_0 + got[0].astype(F32)).astype(BF16)
    out_copy(1, lax.rem(me + n - 1, n), 1).wait_recv()
    out_ref[half:] = (mine_1 + got[1].astype(F32)).astype(BF16)


def per_device(ensemble, reports, report_count, report_cell, report_weight, blending):
    local, cells = ensemble.shape
    n = lax.axis_size("member")
    members = n * local
    slots = reports.shape[1]
    regions, zs = lax.axis_size("region"), Z_CHIPS
    points = report_weight.shape[1]
    half = cells // n // 2
    vmem = pl.BlockSpec(memory_space=pltpu.VMEM)
    anywhere = pl.BlockSpec(memory_space=pltpu.HBM)
    dma = pltpu.SemaphoreType.DMA
    return pl.pallas_call(
        kernel,
        out_shape=jax.ShapeDtypeStruct((cells // n, members), BF16),
        in_specs=[anywhere] * 6,
        out_specs=vmem,
        scratch_shapes=[
            pltpu.SMEM((1,), jnp.int32),
            pltpu.VMEM((local, cells), BF16),
            pltpu.VMEM((1, slots), F32),
            pltpu.VMEM((1, slots), jnp.int32),
            pltpu.VMEM((points, slots), F32),
            pltpu.VMEM((4, 2 * half), F32),
            dma((6,)),
            pltpu.VMEM((members, slots), BF16),
            pltpu.VMEM((members, 4 * half), BF16),
            pltpu.VMEM((members, half), BF16),
            pltpu.VMEM((2, 4, 2 * half), F32),
            pltpu.VMEM((regions, local, MARGIN), BF16),
            pltpu.VMEM((local, 2 * MARGIN), BF16),
            pltpu.VMEM((members, 2 * MARGIN), BF16),
            pltpu.VMEM((3, half, members), BF16),
            pltpu.VMEM((2, half, members), BF16),
            pltpu.VMEM((half, MARGIN), F32),
            pltpu.VMEM((local * cells // MARGIN, MARGIN), F32),
            pltpu.VMEM((points, members, members), F32),
            pltpu.VMEM((points, members, members), F32),
            pltpu.VMEM((points, members, members), BF16),
            pltpu.VMEM((members, MARGIN), F32),
            dma((regions // zs,)), dma((regions // zs,)), dma((regions,)), dma((regions,)), dma((zs,)), dma((zs,)),
            pltpu.SemaphoreType.REGULAR((zs,)), dma((n,)), dma((n,)), dma((n,)), dma((n,)), dma((n,)), dma((n,)),
            dma((2,)), dma((2,)), dma((2,)), dma((n,)), dma((3,)), dma((2,)),
        ],
        compiler_params=pltpu.CompilerParams(
            collective_id=0, has_side_effects=True, vmem_limit_bytes=48 * 1024 * 1024
        ),
    )(report_count, *(pltpu.with_memory_space_constraint(v, pltpu.HBM) for v in (ensemble, reports, report_cell, report_weight[0], blending)))


def solution(mesh):
    return jax.shard_map(
        per_device,
        mesh=mesh,
        in_specs=(
            P("member", "region"),
            P("region", None),
            P("region"),
            P("region", None),
            P("region", "member", None),
            P(None, ("region", "member")),
        ),
        out_specs=P(("region", "member"), None),
        check_vma=False,
    )
```

```python
import functools
import math

import jax
import jax.numpy as jnp
from jax import lax
from jax.experimental import pallas as pl
from jax.experimental.pallas import tpu as pltpu
from jax.sharding import PartitionSpec as P

MESH = pl.DeviceIdType.MESH
MARGIN = 128
Z_CHIPS = 4
F32 = jnp.float32
BF16 = jnp.bfloat16


def split(value):
    high = value.astype(BF16)
    low = (value - high.astype(F32)).astype(BF16)
    return high, low


def dot(a, b):
    return jnp.dot(a, b, preferred_element_type=F32)


def dot_nt(a, b):
    return lax.dot_general(a, b, (((1,), (1,)), ((), ())), preferred_element_type=F32)


def dot_tn(a, b):
    return lax.dot_general(a, b, (((0,), (0,)), ((), ())), preferred_element_type=F32)


def kernel(
    count_hbm, ens_hbm, rep_hbm, cell_hbm, rw_hbm, bl_hbm, out_ref,
    count_ref, ens_ref, rep_ref, cell_ref, rw_ref, bl_ref, in_sem,
    at_buf, cells_buf, extra_buf, bl_buf, bord, fwd, picked, sent, got, mix_s,
    wide_ens, x_s, z_s, t_s, forcing_s,
    by_send, by_recv, dn_send, dn_recv, pu_send, pu_recv, ready, at_send, at_recv, ce_send, ce_recv, fw_send, fw_recv,
    bl_send, bl_recv, xs_send, xs_recv, cn_send, cn_recv,
):
    region = lax.axis_index("region")
    me = lax.axis_index("member")
    local, cells = ens_ref.shape
    zs = Z_CHIPS
    n = 16
    members = n * local
    regions = bord.shape[0]
    ys = regions // zs
    y, z = region // zs, region % zs
    half = cells // n // 2
    slots = at_buf.shape[1]
    first = (n - 1 - me) // (n - 1)
    last = me // (n - 1)

    def peer(i):
        return lax.rem(me + i, n)

    later = zs - 1 - z

    def at_row(i, plane):
        return lax.rem(y + i, ys) * zs + plane

    def y_peer(i):
        return at_row(i, z)

    def rows(d):
        return pl.ds(pl.multiple_of(d * local, local), local)

    def remote(src, dst, ss, rs, **where):
        return pltpu.make_async_remote_copy(
            src_ref=src, dst_ref=dst, send_sem=ss, recv_sem=rs, device_id=where, device_id_type=MESH
        )

    own_block = z * ys + y
    edge_hbm = ens_hbm.at[:, pl.ds(0, MARGIN)]
    own_plane = bord.at[pl.ds(z * ys, ys)]

    def y_copy(i):
        return remote(edge_hbm, bord.at[own_block], by_send.at[i], by_recv.at[i], region=y_peer(i))

    def down_copy(t):
        where = at_row(lax.rem(t, ys), z - t // ys)
        return remote(edge_hbm, bord.at[own_block], dn_send.at[t], dn_recv.at[t], region=where)

    def start_down(t, c):
        down_copy(ys * (z - t // ys) + lax.rem(t, ys)).start()
        return c

    def down_arrival(t):
        return remote(edge_hbm, bord.at[own_block], dn_send.at[t], dn_recv.at[t], region=y_peer(1))

    def up_copy(k):
        return remote(own_plane, own_plane, pu_send.at[k], pu_recv.at[k], region=y * zs + z + k)

    def up_arrival(k):
        return remote(own_plane, own_plane, pu_send.at[k], pu_recv.at[k], region=y_peer(1))

    def at_copy(i):
        block = at_buf.at[rows(me)]
        return remote(block, block, at_send.at[i], at_recv.at[i], member=peer(i))

    def cell_start(d):
        return pl.multiple_of(2 * half * d - half + half * ((n - 1 - d) // (n - 1)) - half * (d // (n - 1)), MARGIN)

    def ce_copy(i):
        source = ens_ref.at[:, pl.ds(cell_start(peer(i)), 4 * half)]
        return remote(source, cells_buf.at[rows(me)], ce_send.at[i], ce_recv.at[i], member=peer(i))

    def fw_copy(i):
        return remote(fwd, picked.at[rows(me)], fw_send.at[i], fw_recv.at[i], member=peer(i))

    def started(copy):
        def body(i, c):
            copy(i).start()
            return c
        return body

    def sent_off(copy):
        def body(i, c):
            copy(i).wait_send()
            return c
        return body

    def arrived(copy):
        def body(i, c):
            copy(i).wait_recv()
            return c
        return body

    barrier = pltpu.get_barrier_semaphore()

    def greet(i, c):
        pl.semaphore_signal(barrier, inc=1, device_id={"member": peer(i)}, device_id_type=MESH)
        return c

    def greet_later(t, c):
        where = at_row(lax.rem(t, ys), z + t // ys)
        pl.semaphore_signal(barrier, inc=1, device_id={"region": where}, device_id_type=MESH)
        return c

    def say_ready(k, c):
        pl.semaphore_signal(ready.at[k], inc=1, device_id={"region": y * zs + z - k}, device_id_type=MESH)
        return c

    def greet_y(i, c):
        pl.semaphore_signal(barrier, inc=1, device_id={"region": y_peer(i)}, device_id_type=MESH)
        return c

    lax.fori_loop(1, ys, greet_y, 0)
    lax.fori_loop(1, n, greet, 0)
    loads = [
        pltpu.make_async_copy(source, landed, in_sem.at[i])
        for i, (source, landed) in enumerate((
            (ens_hbm, ens_ref), (cell_hbm, cell_ref), (bl_hbm, bl_ref), (rw_hbm, rw_ref), (rep_hbm, rep_ref), (count_hbm, count_ref)
        ))
    ]
    for load in loads:
        load.start()
    lax.fori_loop(ys, ys + ys * later, greet_later, 0)
    pl.semaphore_wait(barrier, ys + n - 2 + ys * z)
    lax.fori_loop(1, 1 + z, say_ready, 0)
    lax.fori_loop(0, ys * z, start_down, 0)
    lax.fori_loop(1, ys, started(y_copy), 0)
    for load in loads:
        load.wait()
    bord[own_block] = ens_ref[:, pl.ds(0, MARGIN)]

    target = cell_ref[...]
    relative = target - region * cells
    is_local = (relative >= 0) & (relative < cells)
    lane = lax.rem(jnp.where(is_local, relative, 0), MARGIN)
    column = jnp.where(is_local, relative // MARGIN, -1)
    for h in range(cells // MARGIN):
        wide_ens[h * local:(h + 1) * local, :] = ens_ref[:, h * MARGIN:(h + 1) * MARGIN].astype(F32)
    in_column = (lax.broadcasted_iota(jnp.int32, (cells // MARGIN, slots), 0) == column).astype(F32).astype(BF16)
    in_lane = lax.broadcasted_iota(jnp.int32, (MARGIN, slots), 0) == lane
    gathered = []
    for k in range(local):
        values = wide_ens[pl.ds(k, cells // MARGIN, stride=local), :].astype(BF16)
        found = dot_tn(values, in_column)
        gathered.append(jnp.sum(jnp.where(in_lane, found, 0.0), axis=0, keepdims=True))
    at_buf[rows(me), :] = jnp.concatenate(gathered, axis=0).astype(BF16)

    up = remote(bl_ref, bl_buf.at[0], bl_send.at[0], bl_recv.at[0], member=lax.rem(me + 1, n))
    down = remote(bl_ref, bl_buf.at[1], bl_send.at[1], bl_recv.at[1], member=lax.rem(me + n - 1, n))
    up.start()
    down.start()
    lax.fori_loop(1, n, started(at_copy), 0)

    holder = (target // cells).astype(F32)
    s_low = jnp.min(jnp.where(is_local, 1e6, holder), axis=1, keepdims=True)
    s_high = jnp.max(jnp.where(is_local, -1.0, holder), axis=1, keepdims=True)
    wide_low = jnp.broadcast_to(s_low.astype(jnp.int32), (local, MARGIN))
    wide_high = jnp.broadcast_to(s_high.astype(jnp.int32), (local, MARGIN))

    def pick(plane, row, found):
        low, high = found
        block = bord[plane * ys + row].astype(F32)
        at = row * zs + plane
        return jnp.where(wide_low == at, block, low), jnp.where(wide_high == at, block, high)

    def pick_row(i, found):
        y_copy(i).wait_recv()
        return pick(z, lax.rem(y + ys - i, ys), found)

    def send_up(k, c):
        pl.semaphore_wait(ready.at[k], 1)
        up_copy(k).start()
        return c

    def pick_later(t, found):
        down_arrival(t).wait_recv()
        return pick(z + t // ys, lax.rem(y + ys - lax.rem(t, ys), ys), found)

    def pick_earlier(k, found):
        up_arrival(k).wait_recv()
        for row in range(ys):
            found = pick(z - k, row, found)
        return found

    nothing = jnp.zeros((local, MARGIN), F32)
    found = pick(z, y, (nothing, nothing))
    found = lax.fori_loop(1, ys, pick_row, found)
    lax.fori_loop(1, 1 + later, send_up, 0)
    found = lax.fori_loop(ys, ys + ys * later, pick_later, found)
    low, high = lax.fori_loop(1, 1 + z, pick_earlier, found)
    mine = jnp.concatenate([low, high], axis=1).astype(BF16)
    fwd[...] = mine
    picked[rows(me), :] = mine
    lax.fori_loop(1, n, started(fw_copy), 0)
    lax.fori_loop(1, n, started(ce_copy), 0)

    cells_buf[rows(me), :] = ens_ref[:, pl.ds(cell_start(me), 4 * half)]

    def extra_copy(k):
        d = (1, n - 2)[k]
        source = ens_ref.at[:, pl.ds((0, cells - half)[k], half)]
        return remote(source, extra_buf.at[rows(me)], xs_send.at[k], xs_recv.at[me], member=d)

    for k, d in enumerate((1, n - 2)):
        @pl.when(me != d)
        def _():
            extra_copy(k).start()

        @pl.when(me == d)
        def _():
            extra_buf[rows(me), :] = ens_ref[:, pl.ds((0, cells - half)[k], half)]

    within = lax.rem(target, cells)
    key = jnp.where(
        is_local, -1,
        jnp.where(holder == s_low, within, jnp.where(holder == s_high, MARGIN + within, -1)),
    )
    onehot = (lax.broadcasted_iota(jnp.int32, (2 * MARGIN, slots), 0) == key).astype(F32).astype(BF16)
    active = lax.broadcasted_iota(jnp.int32, (1, slots), 1) < count_ref[0]
    weights = jnp.where(active, rw_ref[...], 0.0)
    points = weights.shape[0]
    pair = jnp.concatenate([weights, weights * rep_ref[...]], axis=0)
    by_cell = dot_nt(jnp.concatenate(split(pair), axis=0), onehot)
    by_cell = by_cell[:2 * points] + by_cell[2 * points:]
    cell_weights, cell_reports = by_cell[:points], by_cell[points:]
    padding = jnp.zeros((MARGIN - points, slots), F32)

    lax.fori_loop(1, n, arrived(at_copy), 0)
    at_reports = at_buf[...].astype(F32)
    mean = jnp.sum(at_reports, axis=0, keepdims=True) * (1.0 / members)
    pert = (at_reports - mean).astype(BF16)
    pert_wide = pert.astype(F32)
    departure = jnp.concatenate([weights * (rep_ref[...] - mean), padding], axis=0).astype(BF16)
    forcing_s[...] = dot_nt(pert, departure)
    for q in range(points):
        x_s[q] = dot_nt((pert_wide * weights[q:q + 1]).astype(BF16), pert)

    up.wait_recv()
    down.wait_recv()

    def mixed(values):
        return values * (1.0 / jnp.sum(values, axis=0, keepdims=True))

    own, below, above = mixed(bl_ref[...]), mixed(bl_buf[0]), mixed(bl_buf[1])
    weights_of = [
        below[2:4, half:],
        jnp.where(me == 0, own[0:2, :half], own[2:4, :half]),
        jnp.where(me == n - 1, own[2:4, half:], own[0:2, half:]),
        above[0:2, :half],
        jnp.where(me == 1, below[2:4, :half], above[0:2, half:]),
    ]
    stacked = jnp.concatenate(weights_of + [jnp.zeros((MARGIN - 10, half), F32)], axis=0)
    mix_s[...] = stacked.T

    lax.fori_loop(1, n, arrived(fw_copy), 0)
    values = picked[...].astype(F32)
    mean = jnp.sum(values, axis=0, keepdims=True) * (1.0 / members)
    pert = (values - mean).astype(BF16)
    pert_wide = pert.astype(F32)
    departure = jnp.concatenate([cell_reports - cell_weights * mean, padding[:, :2 * MARGIN]], axis=0).astype(BF16)
    forcing = forcing_s[...] + dot_nt(pert, departure)
    eye = (
        lax.broadcasted_iota(jnp.int32, (members, members), 0)
        == lax.broadcasted_iota(jnp.int32, (members, members), 1)
    ).astype(F32)

    def total(v):
        return jnp.sum(jnp.sum(v, axis=0, keepdims=True), axis=1, keepdims=True)

    block_eye = eye[:MARGIN, :MARGIN]
    frobs, centres = [], []
    for q in range(points):
        weighted = (pert_wide * cell_weights[q:q + 1]).astype(BF16)
        precision_mat = (members - 1.0) * eye + x_s[q] + dot_nt(weighted, pert)
        trace = sum(
            total(precision_mat[k:k + MARGIN, k:k + MARGIN] * block_eye) for k in range(0, members, MARGIN)
        ) * (1.0 / members)
        frob = jnp.sqrt(total(precision_mat * precision_mat))
        x_s[q] = precision_mat * (1.0 / trace) - eye
        frobs.append(frob)
        centres.append(trace / frob)

    gains = [1.0 for _ in frobs]
    for sweep in range(4):
        for q in range(points):
            f_part = x_s[q]
            d = 1.5 - 0.5 * centres[q]
            away = (0.5 * centres[q] / d) * f_part
            narrow = away.astype(BF16)
            if sweep:
                k_part = z_s[q]
                z_s[q] = k_part - away - dot(k_part.astype(BF16), narrow)
            else:
                z_s[q] = -away
            if sweep < 3:
                h_part = f_part - away - dot(f_part.astype(BF16), narrow)
                x_s[q] = h_part - away - dot(h_part.astype(BF16), narrow)
            gains[q] = gains[q] * d
            centres[q] = centres[q] * d * d
    for q in range(points):
        root = eye + z_s[q]
        frob, gain = frobs[q], gains[q]
        step = jnp.sum(root * forcing[:, q:q + 1], axis=0, keepdims=True)
        mean_weights = jnp.sum(root * step, axis=1, keepdims=True) * (gain * gain / frob)
        t_s[q] = (mean_weights + (math.sqrt(members - 1.0) * gain * lax.rsqrt(frob)) * root).astype(BF16)

    lax.fori_loop(1, n, arrived(ce_copy), 0)

    def turn(values):
        across = values.astype(F32).T
        mean = jnp.sum(across, axis=1, keepdims=True) * (1.0 / members)
        return mean, (across - mean).astype(BF16)

    mix = mix_s[...]

    narrow, wide = 3 * half // 8, 5 * half // 8

    def blended(values, b):
        w0, w1 = mix[:, 2 * b:2 * b + 1], mix[:, 2 * b + 1:2 * b + 2]
        s0 = dot(values[:narrow], t_s[0])
        s1 = dot(values[:wide], t_s[1])
        s2 = dot(values[narrow:], t_s[2])
        s3 = dot(values[wide:], t_s[3])
        return jnp.concatenate([
            w0[:narrow] * s0 + w1[:narrow] * s1[:narrow],
            w0[narrow:wide] * s1[narrow:] + w1[narrow:wide] * s2[:wide - narrow],
            w0[wide:] * s2[wide - narrow:] + w1[wide:] * s3,
        ], axis=0)

    base = pl.multiple_of(half * (1 - first + last), half)

    def part(offset):
        return pl.ds(pl.multiple_of(base + offset, half), half)

    def out_copy(k, d, side):
        return remote(sent.at[k], got.at[side], cn_send.at[k], cn_recv.at[side], member=d)

    @pl.when(me < n - 1)
    def _():
        sent[0] = blended(turn(cells_buf[:, part(2 * half)])[1], 3).astype(BF16)
        out_copy(0, me + 1, 0).start()

    @pl.when(me > 0)
    def _():
        sent[1] = blended(turn(cells_buf[:, part(-half)])[1], 0).astype(BF16)
        out_copy(1, me - 1, 1).start()

    for k, d, target_d, side in ((0, 1, 0, 0), (1, n - 2, n - 1, 1)):
        @pl.when(me == d)
        def _():
            def extra_in(i, c):
                src = peer(i)
                remote(
                    ens_ref.at[:, pl.ds(0, half)], extra_buf.at[rows(src)], xs_send.at[k], xs_recv.at[src], member=src
                ).wait_recv()
                return c

            lax.fori_loop(1, n, extra_in, 0)
            sent[2] = blended(turn(extra_buf[...])[1], 4).astype(BF16)
            out_copy(2, target_d, side).start()

    cell_mean, anomaly = turn(cells_buf[:, part(0)])
    mine_0 = cell_mean + blended(anomaly, 1)
    cell_mean, anomaly = turn(cells_buf[:, part(half)])
    mine_1 = cell_mean + blended(anomaly, 2)

    lax.fori_loop(1, ys, sent_off(y_copy), 0)
    lax.fori_loop(ys, ys + ys * z, sent_off(down_copy), 0)
    lax.fori_loop(1, 1 + later, sent_off(up_copy), 0)
    lax.fori_loop(1, n, sent_off(at_copy), 0)
    lax.fori_loop(1, n, sent_off(fw_copy), 0)
    lax.fori_loop(1, n, sent_off(ce_copy), 0)
    up.wait_send()
    down.wait_send()
    for k, d in enumerate((1, n - 2)):
        @pl.when(me != d)
        def _():
            extra_copy(k).wait_send()

        @pl.when(me == d)
        def _():
            out_copy(2, 0, 0).wait_send()

    @pl.when(me < n - 1)
    def _():
        out_copy(0, me + 1, 0).wait_send()

    @pl.when(me > 0)
    def _():
        out_copy(1, me - 1, 1).wait_send()

    out_copy(0, lax.rem(me + 1, n), 0).wait_recv()
    out_ref[:half] = (mine_0 + got[0].astype(F32)).astype(BF16)
    out_copy(1, lax.rem(me + n - 1, n), 1).wait_recv()
    out_ref[half:] = (mine_1 + got[1].astype(F32)).astype(BF16)


def per_device(ensemble, reports, report_count, report_cell, report_weight, blending):
    local, cells = ensemble.shape
    n = lax.axis_size("member")
    members = n * local
    slots = reports.shape[1]
    regions, zs = lax.axis_size("region"), Z_CHIPS
    points = report_weight.shape[1]
    half = cells // n // 2
    vmem = pl.BlockSpec(memory_space=pltpu.VMEM)
    anywhere = pl.BlockSpec(memory_space=pltpu.HBM)
    dma = pltpu.SemaphoreType.DMA
    return pl.pallas_call(
        kernel,
        out_shape=jax.ShapeDtypeStruct((cells // n, members), BF16),
        in_specs=[anywhere] * 6,
        out_specs=vmem,
        scratch_shapes=[
            pltpu.SMEM((1,), jnp.int32),
            pltpu.VMEM((local, cells), BF16),
            pltpu.VMEM((1, slots), F32),
            pltpu.VMEM((1, slots), jnp.int32),
            pltpu.VMEM((points, slots), F32),
            pltpu.VMEM((4, 2 * half), F32),
            dma((6,)),
            pltpu.VMEM((members, slots), BF16),
            pltpu.VMEM((members, 4 * half), BF16),
            pltpu.VMEM((members, half), BF16),
            pltpu.VMEM((2, 4, 2 * half), F32),
            pltpu.VMEM((regions, local, MARGIN), BF16),
            pltpu.VMEM((local, 2 * MARGIN), BF16),
            pltpu.VMEM((members, 2 * MARGIN), BF16),
            pltpu.VMEM((3, half, members), BF16),
            pltpu.VMEM((2, half, members), BF16),
            pltpu.VMEM((half, MARGIN), F32),
            pltpu.VMEM((local * cells // MARGIN, MARGIN), F32),
            pltpu.VMEM((points, members, members), F32),
            pltpu.VMEM((points, members, members), F32),
            pltpu.VMEM((points, members, members), BF16),
            pltpu.VMEM((members, MARGIN), F32),
            dma((regions // zs,)), dma((regions // zs,)), dma((regions,)), dma((regions,)), dma((zs,)), dma((zs,)),
            pltpu.SemaphoreType.REGULAR((zs,)), dma((n,)), dma((n,)), dma((n,)), dma((n,)), dma((n,)), dma((n,)),
            dma((2,)), dma((2,)), dma((2,)), dma((n,)), dma((3,)), dma((2,)),
        ],
        compiler_params=pltpu.CompilerParams(
            collective_id=0, has_side_effects=True, vmem_limit_bytes=48 * 1024 * 1024
        ),
    )(report_count, *(pltpu.with_memory_space_constraint(v, pltpu.HBM) for v in (ensemble, reports, report_cell, report_weight[0], blending)))


def solution(mesh):
    return jax.shard_map(
        per_device,
        mesh=mesh,
        in_specs=(
            P("member", "region"),
            P("region", None),
            P("region"),
            P("region", None),
            P("region", "member", None),
            P(None, ("region", "member")),
        ),
        out_specs=P(("region", "member"), None),
        check_vma=False,
    )
```

```python
import functools
import math

import jax
import jax.numpy as jnp
from jax import lax
from jax.experimental import pallas as pl
from jax.experimental.pallas import tpu as pltpu
from jax.sharding import PartitionSpec as P

MESH = pl.DeviceIdType.MESH
MARGIN = 128
Z_CHIPS = 4
F32 = jnp.float32
BF16 = jnp.bfloat16


def split(value):
    high = value.astype(BF16)
    low = (value - high.astype(F32)).astype(BF16)
    return high, low


def dot(a, b):
    return jnp.dot(a, b, preferred_element_type=F32)


def dot_nt(a, b):
    return lax.dot_general(a, b, (((1,), (1,)), ((), ())), preferred_element_type=F32)


def dot_tn(a, b):
    return lax.dot_general(a, b, (((0,), (0,)), ((), ())), preferred_element_type=F32)


def kernel(
    count_hbm, ens_hbm, rep_hbm, cell_hbm, rw_hbm, bl_hbm, out_ref,
    count_ref, ens_ref, rep_ref, cell_ref, rw_ref, bl_ref, in_sem,
    at_buf, cells_buf, extra_buf, bl_buf, bord, fwd, picked, sent, got, mix_s,
    wide_ens, x_s, z_s, t_s, forcing_s,
    by_send, by_recv, dn_send, dn_recv, pu_send, pu_recv, ready, at_send, at_recv, ce_send, ce_recv, fw_send, fw_recv,
    bl_send, bl_recv, xs_send, xs_recv, cn_send, cn_recv,
):
    region = lax.axis_index("region")
    me = lax.axis_index("member")
    local, cells = ens_ref.shape
    zs = Z_CHIPS
    n = 16
    members = n * local
    regions = bord.shape[0]
    ys = regions // zs
    y, z = region // zs, region % zs
    half = cells // n // 2
    slots = at_buf.shape[1]
    first = (n - 1 - me) // (n - 1)
    last = me // (n - 1)

    def peer(i):
        return lax.rem(me + i, n)

    later = zs - 1 - z
    early = 1 + n // 2 * (later // (zs - 1))

    def at_row(i, plane):
        return lax.rem(y + i, ys) * zs + plane

    def y_peer(i):
        return at_row(i, z)

    def rows(d):
        return pl.ds(pl.multiple_of(d * local, local), local)

    def remote(src, dst, ss, rs, **where):
        return pltpu.make_async_remote_copy(
            src_ref=src, dst_ref=dst, send_sem=ss, recv_sem=rs, device_id=where, device_id_type=MESH
        )

    own_block = z * ys + y
    edge_hbm = ens_hbm.at[:, pl.ds(0, MARGIN)]
    own_plane = bord.at[pl.ds(z * ys, ys)]

    def y_copy(i):
        return remote(edge_hbm, bord.at[own_block], by_send.at[i], by_recv.at[i], region=y_peer(i))

    def down_copy(t):
        where = at_row(lax.rem(t, ys), z - t // ys)
        return remote(edge_hbm, bord.at[own_block], dn_send.at[t], dn_recv.at[t], region=where)

    def start_down(t, c):
        down_copy(ys * (z - t // ys) + lax.rem(t, ys)).start()
        return c

    def down_arrival(t):
        return remote(edge_hbm, bord.at[own_block], dn_send.at[t], dn_recv.at[t], region=y_peer(1))

    def up_copy(k):
        return remote(own_plane, own_plane, pu_send.at[k], pu_recv.at[k], region=y * zs + z + k)

    def up_arrival(k):
        return remote(own_plane, own_plane, pu_send.at[k], pu_recv.at[k], region=y_peer(1))

    def at_copy(i):
        block = at_buf.at[rows(me)]
        return remote(block, block, at_send.at[i], at_recv.at[i], member=peer(i))

    def cell_start(d):
        return pl.multiple_of(2 * half * d - half + half * ((n - 1 - d) // (n - 1)) - half * (d // (n - 1)), MARGIN)

    def ce_copy(i):
        source = ens_ref.at[:, pl.ds(cell_start(peer(i)), 4 * half)]
        return remote(source, cells_buf.at[rows(me)], ce_send.at[i], ce_recv.at[i], member=peer(i))

    def fw_copy(i):
        return remote(fwd, picked.at[rows(me)], fw_send.at[i], fw_recv.at[i], member=peer(i))

    def started(copy):
        def body(i, c):
            copy(i).start()
            return c
        return body

    def sent_off(copy):
        def body(i, c):
            copy(i).wait_send()
            return c
        return body

    def arrived(copy):
        def body(i, c):
            copy(i).wait_recv()
            return c
        return body

    barrier = pltpu.get_barrier_semaphore()

    def greet(i, c):
        pl.semaphore_signal(barrier, inc=1, device_id={"member": peer(i)}, device_id_type=MESH)
        return c

    def greet_later(t, c):
        where = at_row(lax.rem(t, ys), z + t // ys)
        pl.semaphore_signal(barrier, inc=1, device_id={"region": where}, device_id_type=MESH)
        return c

    def say_ready(k, c):
        pl.semaphore_signal(ready.at[k], inc=1, device_id={"region": y * zs + z - k}, device_id_type=MESH)
        return c

    def greet_y(i, c):
        pl.semaphore_signal(barrier, inc=1, device_id={"region": y_peer(i)}, device_id_type=MESH)
        return c

    lax.fori_loop(1, ys, greet_y, 0)
    lax.fori_loop(1, n, greet, 0)
    loads = [
        pltpu.make_async_copy(source, landed, in_sem.at[i])
        for i, (source, landed) in enumerate((
            (ens_hbm, ens_ref), (cell_hbm, cell_ref), (bl_hbm, bl_ref), (rw_hbm, rw_ref), (rep_hbm, rep_ref), (count_hbm, count_ref)
        ))
    ]
    for load in loads:
        load.start()
    lax.fori_loop(ys, ys + ys * later, greet_later, 0)
    pl.semaphore_wait(barrier, ys + n - 2 + ys * z)
    lax.fori_loop(1, 1 + z, say_ready, 0)
    lax.fori_loop(0, ys * z, start_down, 0)
    lax.fori_loop(1, ys, started(y_copy), 0)
    for load in loads:
        load.wait()
    bord[own_block] = ens_ref[:, pl.ds(0, MARGIN)]

    target = cell_ref[...]
    relative = target - region * cells
    is_local = (relative >= 0) & (relative < cells)
    lane = lax.rem(jnp.where(is_local, relative, 0), MARGIN)
    column = jnp.where(is_local, relative // MARGIN, -1)
    for h in range(cells // MARGIN):
        wide_ens[h * local:(h + 1) * local, :] = ens_ref[:, h * MARGIN:(h + 1) * MARGIN].astype(F32)
    in_column = (lax.broadcasted_iota(jnp.int32, (cells // MARGIN, slots), 0) == column).astype(F32).astype(BF16)
    in_lane = lax.broadcasted_iota(jnp.int32, (MARGIN, slots), 0) == lane
    gathered = []
    for k in range(local):
        values = wide_ens[pl.ds(k, cells // MARGIN, stride=local), :].astype(BF16)
        found = dot_tn(values, in_column)
        gathered.append(jnp.sum(jnp.where(in_lane, found, 0.0), axis=0, keepdims=True))
    at_buf[rows(me), :] = jnp.concatenate(gathered, axis=0).astype(BF16)

    up = remote(bl_ref, bl_buf.at[0], bl_send.at[0], bl_recv.at[0], member=lax.rem(me + 1, n))
    down = remote(bl_ref, bl_buf.at[1], bl_send.at[1], bl_recv.at[1], member=lax.rem(me + n - 1, n))
    up.start()
    down.start()
    lax.fori_loop(1, n, started(at_copy), 0)
    lax.fori_loop(1, early, started(ce_copy), 0)

    holder = (target // cells).astype(F32)
    s_low = jnp.min(jnp.where(is_local, 1e6, holder), axis=1, keepdims=True)
    s_high = jnp.max(jnp.where(is_local, -1.0, holder), axis=1, keepdims=True)
    wide_low = jnp.broadcast_to(s_low.astype(jnp.int32), (local, MARGIN))
    wide_high = jnp.broadcast_to(s_high.astype(jnp.int32), (local, MARGIN))

    def pick(plane, row, found):
        low, high = found
        block = bord[plane * ys + row].astype(F32)
        at = row * zs + plane
        return jnp.where(wide_low == at, block, low), jnp.where(wide_high == at, block, high)

    def pick_row(i, found):
        y_copy(i).wait_recv()
        return pick(z, lax.rem(y + ys - i, ys), found)

    def send_up(k, c):
        pl.semaphore_wait(ready.at[k], 1)
        up_copy(k).start()
        return c

    def pick_later(t, found):
        down_arrival(t).wait_recv()
        return pick(z + t // ys, lax.rem(y + ys - lax.rem(t, ys), ys), found)

    def pick_earlier(k, found):
        up_arrival(k).wait_recv()
        for row in range(ys):
            found = pick(z - k, row, found)
        return found

    nothing = jnp.zeros((local, MARGIN), F32)
    found = pick(z, y, (nothing, nothing))
    found = lax.fori_loop(1, ys, pick_row, found)
    lax.fori_loop(1, 1 + later, send_up, 0)
    found = lax.fori_loop(ys, ys + ys * later, pick_later, found)
    low, high = lax.fori_loop(1, 1 + z, pick_earlier, found)
    mine = jnp.concatenate([low, high], axis=1).astype(BF16)
    fwd[...] = mine
    picked[rows(me), :] = mine
    lax.fori_loop(1, n, started(fw_copy), 0)
    lax.fori_loop(early, n, started(ce_copy), 0)

    cells_buf[rows(me), :] = ens_ref[:, pl.ds(cell_start(me), 4 * half)]

    def extra_copy(k):
        d = (1, n - 2)[k]
        source = ens_ref.at[:, pl.ds((0, cells - half)[k], half)]
        return remote(source, extra_buf.at[rows(me)], xs_send.at[k], xs_recv.at[me], member=d)

    for k, d in enumerate((1, n - 2)):
        @pl.when(me != d)
        def _():
            extra_copy(k).start()

        @pl.when(me == d)
        def _():
            extra_buf[rows(me), :] = ens_ref[:, pl.ds((0, cells - half)[k], half)]

    within = lax.rem(target, cells)
    key = jnp.where(
        is_local, -1,
        jnp.where(holder == s_low, within, jnp.where(holder == s_high, MARGIN + within, -1)),
    )
    onehot = (lax.broadcasted_iota(jnp.int32, (2 * MARGIN, slots), 0) == key).astype(F32).astype(BF16)
    active = lax.broadcasted_iota(jnp.int32, (1, slots), 1) < count_ref[0]
    weights = jnp.where(active, rw_ref[...], 0.0)
    points = weights.shape[0]
    pair = jnp.concatenate([weights, weights * rep_ref[...]], axis=0)
    by_cell = dot_nt(jnp.concatenate(split(pair), axis=0), onehot)
    by_cell = by_cell[:2 * points] + by_cell[2 * points:]
    cell_weights, cell_reports = by_cell[:points], by_cell[points:]
    padding = jnp.zeros((MARGIN - points, slots), F32)

    lax.fori_loop(1, n, arrived(at_copy), 0)
    at_reports = at_buf[...].astype(F32)
    mean = jnp.sum(at_reports, axis=0, keepdims=True) * (1.0 / members)
    pert = (at_reports - mean).astype(BF16)
    pert_wide = pert.astype(F32)
    departure = jnp.concatenate([weights * (rep_ref[...] - mean), padding], axis=0).astype(BF16)
    forcing_s[...] = dot_nt(pert, departure)
    for q in range(points):
        x_s[q] = dot_nt((pert_wide * weights[q:q + 1]).astype(BF16), pert)

    up.wait_recv()
    down.wait_recv()

    def mixed(values):
        return values * (1.0 / jnp.sum(values, axis=0, keepdims=True))

    own, below, above = mixed(bl_ref[...]), mixed(bl_buf[0]), mixed(bl_buf[1])
    weights_of = [
        below[2:4, half:],
        jnp.where(me == 0, own[0:2, :half], own[2:4, :half]),
        jnp.where(me == n - 1, own[2:4, half:], own[0:2, half:]),
        above[0:2, :half],
        jnp.where(me == 1, below[2:4, :half], above[0:2, half:]),
    ]
    stacked = jnp.concatenate(weights_of + [jnp.zeros((MARGIN - 10, half), F32)], axis=0)
    mix_s[...] = stacked.T

    lax.fori_loop(1, n, arrived(fw_copy), 0)
    values = picked[...].astype(F32)
    mean = jnp.sum(values, axis=0, keepdims=True) * (1.0 / members)
    pert = (values - mean).astype(BF16)
    pert_wide = pert.astype(F32)
    departure = jnp.concatenate([cell_reports - cell_weights * mean, padding[:, :2 * MARGIN]], axis=0).astype(BF16)
    forcing = forcing_s[...] + dot_nt(pert, departure)
    eye = (
        lax.broadcasted_iota(jnp.int32, (members, members), 0)
        == lax.broadcasted_iota(jnp.int32, (members, members), 1)
    ).astype(F32)

    def total(v):
        return jnp.sum(jnp.sum(v, axis=0, keepdims=True), axis=1, keepdims=True)

    block_eye = eye[:MARGIN, :MARGIN]
    frobs, centres = [], []
    for q in range(points):
        weighted = (pert_wide * cell_weights[q:q + 1]).astype(BF16)
        precision_mat = (members - 1.0) * eye + x_s[q] + dot_nt(weighted, pert)
        trace = sum(
            total(precision_mat[k:k + MARGIN, k:k + MARGIN] * block_eye) for k in range(0, members, MARGIN)
        ) * (1.0 / members)
        frob = jnp.sqrt(total(precision_mat * precision_mat))
        x_s[q] = precision_mat * (1.0 / trace) - eye
        frobs.append(frob)
        centres.append(trace / frob)

    gains = [1.0 for _ in frobs]
    for sweep in range(4):
        for q in range(points):
            f_part = x_s[q]
            d = 1.5 - 0.5 * centres[q]
            away = (0.5 * centres[q] / d) * f_part
            narrow = away.astype(BF16)
            if sweep:
                k_part = z_s[q]
                z_s[q] = k_part - away - dot(k_part.astype(BF16), narrow)
            else:
                z_s[q] = -away
            if sweep < 3:
                h_part = f_part - away - dot(f_part.astype(BF16), narrow)
                x_s[q] = h_part - away - dot(h_part.astype(BF16), narrow)
            gains[q] = gains[q] * d
            centres[q] = centres[q] * d * d
    for q in range(points):
        root = eye + z_s[q]
        frob, gain = frobs[q], gains[q]
        step = jnp.sum(root * forcing[:, q:q + 1], axis=0, keepdims=True)
        mean_weights = jnp.sum(root * step, axis=1, keepdims=True) * (gain * gain / frob)
        t_s[q] = (mean_weights + (math.sqrt(members - 1.0) * gain * lax.rsqrt(frob)) * root).astype(BF16)

    lax.fori_loop(1, n, arrived(ce_copy), 0)

    def turn(values):
        across = values.astype(F32).T
        mean = jnp.sum(across, axis=1, keepdims=True) * (1.0 / members)
        return mean, (across - mean).astype(BF16)

    mix = mix_s[...]

    narrow, wide = 3 * half // 8, 5 * half // 8

    def blended(values, b):
        w0, w1 = mix[:, 2 * b:2 * b + 1], mix[:, 2 * b + 1:2 * b + 2]
        s0 = dot(values[:narrow], t_s[0])
        s1 = dot(values[:wide], t_s[1])
        s2 = dot(values[narrow:], t_s[2])
        s3 = dot(values[wide:], t_s[3])
        return jnp.concatenate([
            w0[:narrow] * s0 + w1[:narrow] * s1[:narrow],
            w0[narrow:wide] * s1[narrow:] + w1[narrow:wide] * s2[:wide - narrow],
            w0[wide:] * s2[wide - narrow:] + w1[wide:] * s3,
        ], axis=0)

    base = pl.multiple_of(half * (1 - first + last), half)

    def part(offset):
        return pl.ds(pl.multiple_of(base + offset, half), half)

    def out_copy(k, d, side):
        return remote(sent.at[k], got.at[side], cn_send.at[k], cn_recv.at[side], member=d)

    @pl.when(me < n - 1)
    def _():
        sent[0] = blended(turn(cells_buf[:, part(2 * half)])[1], 3).astype(BF16)
        out_copy(0, me + 1, 0).start()

    @pl.when(me > 0)
    def _():
        sent[1] = blended(turn(cells_buf[:, part(-half)])[1], 0).astype(BF16)
        out_copy(1, me - 1, 1).start()

    for k, d, target_d, side in ((0, 1, 0, 0), (1, n - 2, n - 1, 1)):
        @pl.when(me == d)
        def _():
            def extra_in(i, c):
                src = peer(i)
                remote(
                    ens_ref.at[:, pl.ds(0, half)], extra_buf.at[rows(src)], xs_send.at[k], xs_recv.at[src], member=src
                ).wait_recv()
                return c

            lax.fori_loop(1, n, extra_in, 0)
            sent[2] = blended(turn(extra_buf[...])[1], 4).astype(BF16)
            out_copy(2, target_d, side).start()

    cell_mean, anomaly = turn(cells_buf[:, part(0)])
    mine_0 = cell_mean + blended(anomaly, 1)
    cell_mean, anomaly = turn(cells_buf[:, part(half)])
    mine_1 = cell_mean + blended(anomaly, 2)

    lax.fori_loop(1, ys, sent_off(y_copy), 0)
    lax.fori_loop(ys, ys + ys * z, sent_off(down_copy), 0)
    lax.fori_loop(1, 1 + later, sent_off(up_copy), 0)
    lax.fori_loop(1, n, sent_off(at_copy), 0)
    lax.fori_loop(1, n, sent_off(fw_copy), 0)
    lax.fori_loop(1, n, sent_off(ce_copy), 0)
    up.wait_send()
    down.wait_send()
    for k, d in enumerate((1, n - 2)):
        @pl.when(me != d)
        def _():
            extra_copy(k).wait_send()

        @pl.when(me == d)
        def _():
            out_copy(2, 0, 0).wait_send()

    @pl.when(me < n - 1)
    def _():
        out_copy(0, me + 1, 0).wait_send()

    @pl.when(me > 0)
    def _():
        out_copy(1, me - 1, 1).wait_send()

    out_copy(0, lax.rem(me + 1, n), 0).wait_recv()
    out_ref[:half] = (mine_0 + got[0].astype(F32)).astype(BF16)
    out_copy(1, lax.rem(me + n - 1, n), 1).wait_recv()
    out_ref[half:] = (mine_1 + got[1].astype(F32)).astype(BF16)


def per_device(ensemble, reports, report_count, report_cell, report_weight, blending):
    local, cells = ensemble.shape
    n = lax.axis_size("member")
    members = n * local
    slots = reports.shape[1]
    regions, zs = lax.axis_size("region"), Z_CHIPS
    points = report_weight.shape[1]
    half = cells // n // 2
    vmem = pl.BlockSpec(memory_space=pltpu.VMEM)
    anywhere = pl.BlockSpec(memory_space=pltpu.HBM)
    dma = pltpu.SemaphoreType.DMA
    return pl.pallas_call(
        kernel,
        out_shape=jax.ShapeDtypeStruct((cells // n, members), BF16),
        in_specs=[anywhere] * 6,
        out_specs=vmem,
        scratch_shapes=[
            pltpu.SMEM((1,), jnp.int32),
            pltpu.VMEM((local, cells), BF16),
            pltpu.VMEM((1, slots), F32),
            pltpu.VMEM((1, slots), jnp.int32),
            pltpu.VMEM((points, slots), F32),
            pltpu.VMEM((4, 2 * half), F32),
            dma((6,)),
            pltpu.VMEM((members, slots), BF16),
            pltpu.VMEM((members, 4 * half), BF16),
            pltpu.VMEM((members, half), BF16),
            pltpu.VMEM((2, 4, 2 * half), F32),
            pltpu.VMEM((regions, local, MARGIN), BF16),
            pltpu.VMEM((local, 2 * MARGIN), BF16),
            pltpu.VMEM((members, 2 * MARGIN), BF16),
            pltpu.VMEM((3, half, members), BF16),
            pltpu.VMEM((2, half, members), BF16),
            pltpu.VMEM((half, MARGIN), F32),
            pltpu.VMEM((local * cells // MARGIN, MARGIN), F32),
            pltpu.VMEM((points, members, members), F32),
            pltpu.VMEM((points, members, members), F32),
            pltpu.VMEM((points, members, members), BF16),
            pltpu.VMEM((members, MARGIN), F32),
            dma((regions // zs,)), dma((regions // zs,)), dma((regions,)), dma((regions,)), dma((zs,)), dma((zs,)),
            pltpu.SemaphoreType.REGULAR((zs,)), dma((n,)), dma((n,)), dma((n,)), dma((n,)), dma((n,)), dma((n,)),
            dma((2,)), dma((2,)), dma((2,)), dma((n,)), dma((3,)), dma((2,)),
        ],
        compiler_params=pltpu.CompilerParams(
            collective_id=0, has_side_effects=True, vmem_limit_bytes=48 * 1024 * 1024
        ),
    )(report_count, *(pltpu.with_memory_space_constraint(v, pltpu.HBM) for v in (ensemble, reports, report_cell, report_weight[0], blending)))


def solution(mesh):
    return jax.shard_map(
        per_device,
        mesh=mesh,
        in_specs=(
            P("member", "region"),
            P("region", None),
            P("region"),
            P("region", None),
            P("region", "member", None),
            P(None, ("region", "member")),
        ),
        out_specs=P(("region", "member"), None),
        check_vma=False,
    )
```
